32 devices in a mesh: dp: 4 (over z), expert: 8 (over y, x, core).
Axes of the slice: x: 2, y: 2, z: 4, core: 2. Of those that a mesh axis runs over, the one named last changes fastest.
Arguments:
- tokens: bfloat16 [8, 64, 4096], P('expert'), may hold values from -6 to 6
- norm_gain: float32 [4096], replicated, may hold values from 0.25 to 1.75
- expert_ids: int32 [8, 64, 8], P('expert'), may hold values from 0 to 15, all different within a row; in each aligned block of 64 rows (0 to 63, 64 to 127, ..., all dimensions but the last counted through in order) at most 36 rows name the same one
- route_weights: float32 [8, 64, 8], P('expert'), may hold values from 0.02 to 0.4
- gate_proj: bfloat16 [16, 1536, 4096], P('expert', 'dp'), may hold values from -0.09375 to 0.09375
- up_proj: bfloat16 [16, 1536, 4096], P('expert', 'dp'), may hold values from -0.09375 to 0.09375
- down_proj: bfloat16 [16, 1536, 4096], P('expert', 'dp'), may hold values from -0.15625 to 0.15625
Outputs:
- mixed: bfloat16 [8, 64, 4096], P('expert', 'dp')
The draws below stay inside these ranges and needn't reach their ends.
Inputs may be any that keep to these rules, and one draw needn't show every extreme that they name: `expert_ids`: each token names 8 different experts. Within one group no expert is named by more than 36 tokens, and in every draw some expert is named by exactly 36 tokens of some group.
All inputs are finite; a program needn't handle non-finite values.
Results may differ from the reference program's by a relative error of at most 0.019.
Values may be sent and summed in bfloat16 or wider, within the bound.
A program may use at most 128 MiB of HBM per device.

```python
import math
import jax
import jax.numpy as jnp
import numpy as np
from jax import lax

D = 4096
FF = 1536
TOP = 8
GROUP_TOK = 64
EXPERTS = 16
GROUPS = 8
FF_DEV = 384
MOST = 36


def steps_of(key, extent, shards, low, largest):
    def one(axis_at, shards_of):
        steps = jax.random.uniform(jax.random.fold_in(jax.random.fold_in(key, 6), axis_at), (shards_of,), jnp.float32, low / len(shards), largest / len(shards))
        return jnp.repeat(jnp.exp(steps), extent[axis_at] // shards_of).reshape((-1,) + (1,) * (len(extent) - axis_at - 1))

    loudness = one(*shards[0])
    for cut in shards[1:]:
        loudness = loudness * one(*cut)
    return loudness


def assign_block(rng, own, number, rows, count, top, reach, skew):
    ranking = jax.random.permutation(rng, count)
    heavy_load, common = shares(count, rows * top, reach, skew, True), shares(count, rows * top, reach, skew, False)
    places = jnp.arange(count)

    def named(sizes, rotation):
        used = int((sizes > 0).sum())
        fixed = max(1, used // 4)
        passed = fixed + (places - fixed + rotation * (used - fixed)) % max(1, count - fixed)
        return jnp.zeros((count,), jnp.int32).at[ranking[jnp.where(places < fixed, places, passed)]].set(jnp.asarray(sizes, jnp.int32))

    sizes = jnp.where(number % 4 == 0, named(heavy_load, number // 4), named(common, number - number // 4 - 1))
    mixed = jax.random.permutation(jax.random.fold_in(own, 3), count)
    giver, taker = mixed[0:count // 2 * 2:2], mixed[1:count // 2 * 2:2]
    room = jnp.minimum(sizes[giver] - 1, reach - sizes[taker]) // 2
    room = jnp.where((giver == ranking[0]) | (taker == ranking[0]) | (sizes[taker] == 0), 0, jnp.maximum(room, 0))
    passed = jax.random.randint(jax.random.fold_in(own, 4), (count // 2,), 0, 1 << 20) % (room + 1)
    sizes = sizes.at[giver].add(-passed).at[taker].add(passed)
    members = jnp.searchsorted(jnp.cumsum(sizes), jnp.arange(rows * top), side="right").astype(jnp.int32)
    listing = members.reshape(top, rows).T
    listing = listing[jax.random.permutation(jax.random.fold_in(own, 1), rows)]
    rotation = jax.random.randint(jax.random.fold_in(own, 2), (rows, 1), 0, top)
    return jnp.take_along_axis(listing, (jnp.arange(top)[None, :] + rotation) % top, axis=1)


def shares(number_of, total, reach, lean, full):
    loads = [(1 << 20) // math.isqrt(grade ** lean) + 1 for grade in range(1, number_of + 1)]
    largest = reach if full else min(reach, max(-(-total // number_of), total * loads[0] // sum(loads)))
    least = 1 if total - largest >= number_of - 1 else 0
    holding, spare = [largest] + [least] * (number_of - 1), total - largest - least * (number_of - 1)
    while spare > 0:
        movable = [i for i in range(1, number_of) if holding[i] < largest] or [i for i in range(1, number_of) if holding[i] < reach]
        mass, left = sum([loads[i] for i in movable]), spare
        for i in movable:
            extra = min(reach - holding[i], max(1, left * loads[i] // mass), spare)
            holding[i] = holding[i] + extra
            spare = spare - extra
    return np.array(holding)


def gaussian(rng, dims, width, most, shards=(), kind=jnp.bfloat16):
    result = jax.random.normal(rng, dims, jnp.float32) * width
    if len(shards) > 0:
        result = steps_of(rng, dims, shards, -0.22, 0.18) * result
    return jnp.clip(result, min=-most, max=most).astype(kind)


def setup_inputs(seed: int = 0) -> dict:
    arg_keys = jax.random.split(jax.random.key(seed), 8)
    tokens = gaussian(arg_keys[0], (GROUPS, GROUP_TOK, D), 1.0, 6.0, ((0, 8),))
    norm_gain = jnp.clip(1.0 + 0.15 * jax.random.normal(arg_keys[1], (D,), jnp.float32), 0.25, 1.75)
    expert_ids_keys = jax.random.split(jax.random.fold_in(arg_keys[2], 1), GROUPS * GROUP_TOK // GROUP_TOK)
    expert_ids_turns = jax.random.permutation(jax.random.fold_in(arg_keys[2], 3), GROUPS * GROUP_TOK // GROUP_TOK)
    expert_ids = jax.vmap(lambda own, number: assign_block(jax.random.fold_in(arg_keys[2], 2), own, number, GROUP_TOK, EXPERTS, TOP, MOST, 2))(expert_ids_keys, expert_ids_turns).reshape((GROUPS, GROUP_TOK, TOP))
    route_weights = jnp.clip(jnp.exp(math.log(0.4) - 2.9957323 * jax.random.uniform(arg_keys[3], (GROUPS, GROUP_TOK, TOP), jnp.float32) ** steps_of(arg_keys[3], (GROUPS, GROUP_TOK, TOP), ((0, 8),), -0.2, 0.2)), 0.02, 0.4)
    gate_proj = gaussian(arg_keys[4], (EXPERTS, FF, D), D ** -0.5, 0.09375, ((0, 8), (1, 4)))
    up_proj = gaussian(arg_keys[5], (EXPERTS, FF, D), D ** -0.5, 0.09375, ((0, 8), (1, 4)))
    down_proj = gaussian(arg_keys[6], (EXPERTS, FF, D), FF ** -0.5, 0.15625, ((0, 8), (1, 4)))
    return {"tokens": tokens, "norm_gain": norm_gain, "expert_ids": expert_ids, "route_weights": route_weights, "gate_proj": gate_proj, "up_proj": up_proj, "down_proj": down_proj}


def rank_slots(id_table, expert_total):
    flat_ids = id_table.reshape(-1)
    onehot = (flat_ids[:, None] == jnp.arange(expert_total, dtype=jnp.int32)[None, :]).astype(jnp.int32)
    before = jnp.cumsum(onehot, axis=0) - onehot
    return lax.optimization_barrier(jnp.sum(before * onehot, axis=1)).reshape(id_table.shape).astype(jnp.int32)

def reference(tokens, norm_gain, expert_ids, route_weights, gate_proj, up_proj, down_proj):
    tok_float = tokens.astype(jnp.float32)
    inv_rms = lax.rsqrt(lax.optimization_barrier(jnp.mean(tok_float * tok_float, axis=-1, keepdims=True)) + 1e-06)
    normed = (tok_float * inv_rms * norm_gain.astype(jnp.float32)).astype(jnp.bfloat16)

    def group_ranks(id_table):
        return rank_slots(id_table, EXPERTS)
    slot_rank = jax.vmap(group_ranks)(expert_ids)
    slot_index = (expert_ids * MOST + slot_rank).astype(jnp.int32)
    token_order = jnp.broadcast_to(jnp.arange(GROUP_TOK, dtype=jnp.int32)[:, None], (GROUP_TOK, TOP))

    def build_tables(slot_row, weight_row):
        sources = jnp.full((EXPERTS * MOST,), GROUP_TOK, jnp.int32).at[slot_row.reshape(-1)].set(token_order.reshape(-1))
        slot_weights = jnp.zeros((EXPERTS * MOST,), jnp.float32).at[slot_row.reshape(-1)].set(weight_row.reshape(-1))
        return (sources, slot_weights)
    sources, slot_weights = jax.vmap(build_tables)(slot_index, route_weights)
    sources = sources.reshape(GROUPS, EXPERTS, MOST)
    slot_weights = slot_weights.reshape(GROUPS, EXPERTS, MOST)
    padded = jnp.concatenate([normed, jnp.zeros((GROUPS, 1, D), jnp.bfloat16)], axis=1)
    group_index = jnp.broadcast_to(jnp.arange(GROUPS, dtype=jnp.int32)[:, None], (GROUPS, MOST))
    block_count = FF // FF_DEV

    def one_expert(total, expert_no):
        pick_index = lax.dynamic_index_in_dim(sources, expert_no, axis=1, keepdims=False)
        pick_weights = lax.dynamic_index_in_dim(slot_weights, expert_no, axis=1, keepdims=False)
        rows = padded[group_index, pick_index].reshape(GROUPS * MOST, D).astype(jnp.float32)
        gate_act = jnp.einsum('rd,fd->rf', rows, gate_proj[expert_no].astype(jnp.float32), precision=lax.Precision.HIGHEST)
        up_act = jnp.einsum('rd,fd->rf', rows, up_proj[expert_no].astype(jnp.float32), precision=lax.Precision.HIGHEST)
        hidden = lax.optimization_barrier((jax.nn.silu(gate_act) * up_act).astype(jnp.bfloat16)).astype(jnp.float32)
        hidden_blocks = hidden.reshape(GROUPS * MOST, block_count, FF_DEV)
        down_blocks = down_proj[expert_no].astype(jnp.float32).reshape(block_count, FF_DEV, D)
        partial_value = jnp.einsum('rpf,pfd->rpd', hidden_blocks, down_blocks, precision=lax.Precision.HIGHEST)
        partial_value = lax.optimization_barrier(partial_value.astype(jnp.bfloat16)).astype(jnp.float32)
        summed = lax.optimization_barrier(jnp.sum(partial_value, axis=1)).reshape(GROUPS, MOST, D) * pick_weights[:, :, None]
        total = total.at[group_index, pick_index].add(summed, mode='drop')
        return (total, None)
    total_sum, ignored = lax.scan(one_expert, jnp.zeros((GROUPS, GROUP_TOK, D), jnp.float32), jnp.arange(EXPERTS, dtype=jnp.int32))
    return total_sum.astype(jnp.bfloat16)
```

```python
import functools

import jax
import jax.numpy as jnp
from jax import lax
from jax.experimental import pallas as pl
from jax.experimental.pallas import tpu as pltpu
from jax.sharding import PartitionSpec as P

MESH = pl.DeviceIdType.MESH
CHUNKS = 4
OWN, ALONG_X, ALONG_Y, DIAGONAL, SIBLING = 0, 1, 2, 3, 4


def fused(
    dp_count,
    local_experts,
    tok_ref,
    gain_ref,
    dense_ref,
    gate_hbm,
    up_hbm,
    down_hbm,
    out_ref,
    w_in,
    w_out,
    rows,
    dense,
    acc,
    hidden,
    to_sib,
    kept,
    from_sib,
    to_x,
    to_y,
    from_x,
    from_y,
    to_x2,
    to_y2,
    from_x2,
    from_y2,
    summed,
    to_z,
    from_z,
    w_sem,
    d_send,
    d_recv,
    a_send,
    a_recv,
    r_send,
    r_recv,
):
    me = lax.axis_index("expert")
    plane = lax.axis_index("dp")
    sib = me + 1 - 2 * lax.rem(me, 2)
    nx = me + 2 - 4 * lax.rem(me // 2, 2)
    ny = me + 4 - 8 * (me // 4)
    token_count, width = tok_ref.shape
    span = width // CHUNKS
    half = token_count // 2
    own = token_count // dp_count
    hid = w_out.shape[0]
    all_rows = 8 * token_count
    core_rows = 4 * token_count

    loads = [
        pltpu.make_async_copy(gate_hbm, w_in.at[pl.ds(0, hid)], w_sem.at[0]),
        pltpu.make_async_copy(up_hbm, w_in.at[pl.ds(hid, hid)], w_sem.at[1]),
        pltpu.make_async_copy(down_hbm, w_out, w_sem.at[2]),
    ]
    for load in loads:
        load.start()

    barrier = pltpu.get_barrier_semaphore()
    for peer in (sib, nx, ny):
        pl.semaphore_signal(barrier, inc=1, device_id={"expert": peer}, device_id_type=MESH)
    for step in range(1, dp_count):
        pl.semaphore_signal(
            barrier,
            inc=1,
            device_id={"dp": lax.rem(plane + step, dp_count)},
            device_id_type=MESH,
        )

    tok = tok_ref[...].astype(jnp.float32)
    inv_rms = lax.rsqrt(jnp.mean(tok * tok, axis=-1, keepdims=True) + 1e-06)
    for c in range(CHUNKS):
        cols = slice(c * span, (c + 1) * span)
        part = tok_ref[:, cols].astype(jnp.float32) * inv_rms * gain_ref[:, cols]
        rows[c, OWN] = part.astype(jnp.bfloat16)
    dense[OWN] = dense_ref[...]

    pl.semaphore_wait(barrier, 3 + dp_count - 1)

    def push(src, dst, send, recv, **where):
        return pltpu.make_async_remote_copy(
            src_ref=src,
            dst_ref=dst,
            send_sem=send,
            recv_sem=recv,
            device_id=where,
            device_id_type=MESH,
        )

    def dense_push(k, src, dst, peer):
        return push(dense.at[src], dense.at[dst], d_send.at[k], d_recv.at[k], expert=peer)

    dense_copies = [
        dense_push(0, OWN, ALONG_X, nx),
        dense_push(1, OWN, ALONG_Y, ny),
        dense_push(2, OWN, SIBLING, sib),
        dense_push(3, ALONG_X, DIAGONAL, ny),
        dense_push(4, ALONG_X, SIBLING + ALONG_X, sib),
        dense_push(5, ALONG_Y, SIBLING + ALONG_Y, sib),
        dense_push(6, DIAGONAL, SIBLING + DIAGONAL, sib),
    ]

    def gather_copies(c):
        def go(k, src, dst, peer, part=None):
            a, b = rows.at[c, src], rows.at[c, dst]
            if part is not None:
                a = rows.at[c, src, pl.ds(part * half, half)]
                b = rows.at[c, dst, pl.ds(part * half, half)]
            return push(a, b, a_send.at[c, k], a_recv.at[c, k], expert=peer)

        return [
            go(0, OWN, ALONG_X, nx),
            go(1, OWN, ALONG_Y, ny),
            go(2, OWN, SIBLING, sib),
            go(3, ALONG_X, DIAGONAL, ny, 0),
            go(4, ALONG_Y, DIAGONAL, nx, 1),
            go(5, ALONG_X, SIBLING + ALONG_X, sib),
            go(6, ALONG_Y, SIBLING + ALONG_Y, sib),
            go(7, DIAGONAL, SIBLING + DIAGONAL, sib),
        ]

    gather = [gather_copies(c) for c in range(CHUNKS)]
    for k in range(3):
        dense_copies[k].start()
    for c in range(CHUNKS):
        for k in range(3):
            gather[c][k].start()

    acc[...] = jnp.zeros_like(acc)

    def forward(c):
        gather[c][0].wait_recv()
        gather[c][3].start()
        gather[c][5].start()
        gather[c][1].wait_recv()
        gather[c][4].start()
        gather[c][6].start()

    def forward_diagonal(c):
        gather[c][3].wait_recv()
        gather[c][4].wait_recv()
        gather[c][7].start()

    def multiply_in(c):
        for k in (2, 5, 6, 7):
            gather[c][k].wait_recv()

        @pl.loop(0, acc.shape[0])
        def _(t):
            tile = acc.shape[2]
            w = w_in[pl.ds(pl.multiple_of(t * tile, tile), tile), c * span : (c + 1) * span]
            x = rows[c].reshape(all_rows, span)
            acc[t] += lax.dot_general(
                x, w, (((1,), (1,)), ((), ())), preferred_element_type=jnp.float32
            )

    forward(0)
    dense_copies[0].wait_recv()
    dense_copies[3].start()
    dense_copies[4].start()
    dense_copies[1].wait_recv()
    dense_copies[5].start()
    forward(1)
    forward_diagonal(0)
    dense_copies[3].wait_recv()
    dense_copies[6].start()
    loads[0].wait()
    loads[1].wait()
    multiply_in(0)
    forward(2)
    forward_diagonal(1)
    multiply_in(1)
    forward(3)
    forward_diagonal(2)
    multiply_in(2)
    forward_diagonal(3)
    for k in (2, 4, 5, 6):
        dense_copies[k].wait_recv()
    multiply_in(3)

    expert_rows = lax.broadcasted_iota(jnp.int32, dense.shape[1:], 0)
    diagonal = lax.broadcasted_iota(
        jnp.int32, (token_count, dense.shape[2]), 0
    ) == lax.broadcasted_iota(jnp.int32, (token_count, dense.shape[2]), 1)
    tiles = acc.shape[0] // 2
    tile = acc.shape[2]
    lanes = 128
    per_expert = hid // local_experts
    for p in range(8):
        at = slice(p * token_count, (p + 1) * token_count)
        scales = []
        for j in range(local_experts):
            row = jnp.sum(
                jnp.where(expert_rows == me * local_experts + j, dense[p], 0.0),
                axis=0,
                keepdims=True,
            )
            scales.append(jnp.sum(jnp.where(diagonal, row, 0.0), axis=1, keepdims=True))
        for k in range(hid // lanes):
            t, inner = (k * lanes) // tile, (k * lanes) % tile
            g = acc[t, at, inner : inner + lanes]
            u = acc[tiles + t, at, inner : inner + lanes]
            h = g / (1.0 + jnp.exp(-g)) * u * scales[(k * lanes) // per_expert]
            hidden[at, k * lanes : (k + 1) * lanes] = h.astype(jnp.bfloat16)

    def reduce_copies(n):
        def go(k, src, dst, **where):
            return push(src, dst, r_send.at[n, k], r_recv.at[n, k], **where)

        copies = [
            go(0, to_sib.at[n], from_sib.at[n], expert=sib),
            go(1, to_x.at[n], from_x.at[n], expert=nx),
            go(2, to_y.at[n], from_y.at[n], expert=ny),
            go(3, to_y2.at[n], from_y2.at[n], expert=ny),
            go(4, to_x2.at[n], from_x2.at[n], expert=nx),
        ]
        for step in range(1, dp_count):
            peer = lax.rem(plane + step, dp_count)
            copies.append(go(4 + step, to_z.at[n, peer], from_z.at[n, step - 1], dp=peer))
        return copies

    reduce = [reduce_copies(n) for n in range(CHUNKS)]

    def multiply_out(n):
        step = 256

        @pl.loop(0, span // step)
        def _(t):
            w = w_out[:, pl.ds(pl.multiple_of(n * span + t * step, step), step)]
            y = jnp.dot(hidden[...], w, preferred_element_type=jnp.float32)
            cols = pl.ds(pl.multiple_of(t * step, step), step)
            to_sib[n, :, cols] = y[core_rows:].astype(jnp.bfloat16)
            kept[n, :, cols] = y[:core_rows]

        reduce[n][0].start()

    def block(place, part):
        return slice(place * token_count + part * half, place * token_count + (part + 1) * half)

    def pair_sum(n):
        reduce[n][0].wait_recv()

        def total(place, part):
            at = block(place, part)
            return kept[n, at] + from_sib[n, at].astype(jnp.float32)

        to_x[n, :half] = total(ALONG_X, 0).astype(jnp.bfloat16)
        to_x[n, half:] = total(DIAGONAL, 0).astype(jnp.bfloat16)
        reduce[n][1].start()
        to_y[n, :half] = total(ALONG_Y, 1).astype(jnp.bfloat16)
        to_y[n, half:] = total(DIAGONAL, 1).astype(jnp.bfloat16)
        reduce[n][2].start()
        for place, part in ((OWN, 0), (OWN, 1), (ALONG_Y, 0), (ALONG_X, 1)):
            kept[n, block(place, part)] = total(place, part)

    def second_hop(n):
        reduce[n][1].wait_recv()
        to_y2[n] = (
            kept[n, block(ALONG_Y, 0)] + from_x[n, half:].astype(jnp.float32)
        ).astype(jnp.bfloat16)
        reduce[n][3].start()
        reduce[n][2].wait_recv()
        to_x2[n] = (
            kept[n, block(ALONG_X, 1)] + from_y[n, half:].astype(jnp.float32)
        ).astype(jnp.bfloat16)
        reduce[n][4].start()

    def across_planes(n):
        reduce[n][3].wait_recv()
        reduce[n][4].wait_recv()
        first = (
            kept[n, block(OWN, 0)]
            + from_x[n, :half].astype(jnp.float32)
            + from_y2[n].astype(jnp.float32)
        )
        second = (
            kept[n, block(OWN, 1)]
            + from_y[n, :half].astype(jnp.float32)
            + from_x2[n].astype(jnp.float32)
        )
        per_half = half // own
        for i in range(per_half):
            at = slice(i * own, (i + 1) * own)
            summed[n, i] = first[at]
            summed[n, per_half + i] = second[at]
            to_z[n, i] = first[at].astype(jnp.bfloat16)
            to_z[n, per_half + i] = second[at].astype(jnp.bfloat16)
        for step in range(1, dp_count):
            reduce[n][4 + step].start()

    def finish(n):
        result = summed[n, plane]
        for step in range(1, dp_count):
            reduce[n][4 + step].wait_recv()
            result = result + from_z[n, step - 1].astype(jnp.float32)
        out_ref[:, n * span : (n + 1) * span] = result.astype(jnp.bfloat16)

    loads[2].wait()
    multiply_out(0)
    multiply_out(1)
    pair_sum(0)
    multiply_out(2)
    pair_sum(1)
    multiply_out(3)
    pair_sum(2)
    second_hop(0)
    pair_sum(3)
    second_hop(1)
    across_planes(0)
    second_hop(2)
    across_planes(1)
    second_hop(3)
    across_planes(2)
    finish(0)
    across_planes(3)
    finish(1)
    finish(2)
    finish(3)

    for copy in dense_copies:
        copy.wait_send()
    for copies in gather + reduce:
        for copy in copies:
            copy.wait_send()


def fused_body(tokens, norm_gain, expert_ids, route_weights, gate_proj, up_proj, down_proj):
    dp_count = lax.axis_size("dp")
    local_experts, block_hid, width = gate_proj.shape
    experts = local_experts * lax.axis_size("expert")
    token_count = tokens.shape[1]
    hid = local_experts * block_hid
    span = width // CHUNKS
    half = token_count // 2
    own = token_count // dp_count
    core_rows = 4 * token_count
    tile = 256

    named = expert_ids[0].T[None] == jnp.arange(experts, dtype=jnp.int32)[:, None, None]
    dense = jnp.sum(jnp.where(named, route_weights[0].T[None], 0.0), axis=1)
    dense = jnp.pad(dense, ((0, 0), (0, 128 - token_count)))

    bf16, f32 = jnp.bfloat16, jnp.float32
    vmem = pl.BlockSpec(memory_space=pltpu.VMEM)
    anywhere = pl.BlockSpec(memory_space=pl.ANY)
    dma = pltpu.SemaphoreType.DMA
    mixed = pl.pallas_call(
        functools.partial(fused, dp_count, local_experts),
        out_shape=jax.ShapeDtypeStruct((own, width), bf16),
        in_specs=[vmem] * 3 + [anywhere] * 3,
        out_specs=vmem,
        scratch_shapes=[
            pltpu.VMEM((2 * hid, width), bf16),
            pltpu.VMEM((hid, width), bf16),
            pltpu.VMEM((CHUNKS, 8, token_count, span), bf16),
            pltpu.VMEM((8, experts, 128), f32),
            pltpu.VMEM((2 * hid // tile, 8 * token_count, tile), f32),
            pltpu.VMEM((8 * token_count, hid), bf16),
            pltpu.VMEM((CHUNKS, core_rows, span), bf16),
            pltpu.VMEM((CHUNKS, core_rows, span), f32),
            pltpu.VMEM((CHUNKS, core_rows, span), bf16),
            pltpu.VMEM((CHUNKS, 2 * half, span), bf16),
            pltpu.VMEM((CHUNKS, 2 * half, span), bf16),
            pltpu.VMEM((CHUNKS, 2 * half, span), bf16),
            pltpu.VMEM((CHUNKS, 2 * half, span), bf16),
            pltpu.VMEM((CHUNKS, half, span), bf16),
            pltpu.VMEM((CHUNKS, half, span), bf16),
            pltpu.VMEM((CHUNKS, half, span), bf16),
            pltpu.VMEM((CHUNKS, half, span), bf16),
            pltpu.VMEM((CHUNKS, dp_count, own, span), f32),
            pltpu.VMEM((CHUNKS, dp_count, own, span), bf16),
            pltpu.VMEM((CHUNKS, dp_count - 1, own, span), bf16),
            dma((3,)),
            dma((7,)),
            dma((7,)),
            dma((CHUNKS, 8)),
            dma((CHUNKS, 8)),
            dma((CHUNKS, 4 + dp_count)),
            dma((CHUNKS, 4 + dp_count)),
        ],
        compiler_params=pltpu.CompilerParams(
            collective_id=0, has_side_effects=True, vmem_limit_bytes=56 * 1024 * 1024
        ),
        cost_estimate=pl.CostEstimate(
            flops=2 * 3 * 8 * token_count * hid * width,
            bytes_accessed=3 * hid * width * 2,
            transcendentals=8 * token_count * hid,
        ),
    )(
        tokens[0],
        norm_gain[None],
        dense,
        gate_proj.reshape(hid, width),
        up_proj.reshape(hid, width),
        down_proj.reshape(hid, width),
    )
    return mixed[None]


def rank_slots(id_table, expert_total):
    flat_ids = id_table.reshape(-1)
    onehot = (flat_ids[:, None] == jnp.arange(expert_total, dtype=jnp.int32)[None, :]).astype(
        jnp.int32
    )
    before = jnp.cumsum(onehot, axis=0) - onehot
    return jnp.sum(before * onehot, axis=1).reshape(id_table.shape)


def body(tokens, norm_gain, expert_ids, route_weights, gate_proj, up_proj, down_proj):
    dp_count = lax.axis_size("dp")
    expert_count = lax.axis_size("expert")
    local_experts = gate_proj.shape[0]
    model_width = tokens.shape[2]
    group_ids = expert_ids[0]
    group_weights = route_weights[0]
    group_size = group_ids.shape[0]
    own_rows = group_size // dp_count
    top_k = group_ids.shape[1]
    experts = local_experts * expert_count
    capacity = dp_count * (group_size * top_k // (experts * dp_count) + 1)
    tok_float = tokens[0].astype(jnp.float32)
    inv_rms = lax.rsqrt(jnp.mean(tok_float * tok_float, axis=-1, keepdims=True) + 1e-06)
    group_rows = (tok_float * inv_rms * norm_gain).astype(jnp.bfloat16)
    slot_rank = rank_slots(group_ids, experts)
    slot_index = group_ids * capacity + slot_rank
    token_order = jnp.broadcast_to(
        jnp.arange(group_size, dtype=jnp.int32)[:, None], (group_size, top_k)
    )
    sources = (
        jnp.full((experts * capacity,), group_size, jnp.int32)
        .at[slot_index.reshape(-1)]
        .set(token_order.reshape(-1))
    )
    padded = jnp.concatenate([group_rows, jnp.zeros((1, model_width), jnp.bfloat16)], axis=0)
    outgoing = jnp.take(padded, sources, axis=0).reshape(
        expert_count, local_experts, capacity, model_width
    )
    incoming = lax.all_to_all(outgoing, "expert", split_axis=0, concat_axis=0, tiled=True)
    gate_act = jnp.einsum("sjmd,jfd->sjmf", incoming, gate_proj, preferred_element_type=jnp.float32)
    up_act = jnp.einsum("sjmd,jfd->sjmf", incoming, up_proj, preferred_element_type=jnp.float32)
    hidden = (jax.nn.silu(gate_act) * up_act).astype(jnp.bfloat16)
    partial_rows = jnp.einsum(
        "sjmf,jfd->sjmd", hidden, down_proj, preferred_element_type=jnp.float32
    ).astype(jnp.bfloat16)
    returned = lax.all_to_all(partial_rows, "expert", split_axis=0, concat_axis=0, tiled=True)
    lookup = jnp.concatenate(
        [
            returned.reshape(experts * capacity, model_width),
            jnp.zeros((1, model_width), jnp.bfloat16),
        ],
        axis=0,
    )
    picked = (
        jnp.take(lookup, slot_index.reshape(-1), axis=0)
        .reshape(own_rows * lax.axis_size("dp"), top_k, model_width)
        .astype(jnp.float32)
    )
    mixed = lax.psum_scatter(
        jnp.sum(picked * group_weights[:, :, None], axis=1).astype(jnp.bfloat16),
        "dp",
        scatter_dimension=0,
        tiled=True,
    )
    return mixed[None]


def solution(mesh):
    placed = (
        P("expert", None, None),
        P(),
        P("expert", None, None),
        P("expert", None, None),
        P("expert", "dp", None),
        P("expert", "dp", None),
        P("expert", "dp", None),
    )
    small = mesh.shape["expert"] == 8 and mesh.shape["dp"] == 4
    return jax.shard_map(
        fused_body if small else body, mesh=mesh, in_specs=placed, out_specs=P("expert", "dp", None), check_vma=False
    )
```

```python
import functools

import jax
import jax.numpy as jnp
from jax import lax
from jax.experimental import pallas as pl
from jax.experimental.pallas import tpu as pltpu
from jax.sharding import PartitionSpec as P

MESH = pl.DeviceIdType.MESH
CHUNKS = 4
OWN, ALONG_X, ALONG_Y, DIAGONAL, SIBLING = 0, 1, 2, 3, 4


def fused(
    dp_count,
    local_experts,
    tok_ref,
    gain_ref,
    dense_ref,
    gate_hbm,
    up_hbm,
    down_hbm,
    out_ref,
    w_in,
    w_out,
    rows,
    flipped,
    dense,
    acc,
    hidden,
    to_sib,
    kept,
    from_sib,
    to_x,
    to_y,
    from_x,
    from_y,
    to_x2,
    to_y2,
    from_x2,
    from_y2,
    summed,
    to_z,
    from_z,
    w_sem,
    d_send,
    d_recv,
    a_send,
    a_recv,
    r_send,
    r_recv,
):
    me = lax.axis_index("expert")
    plane = lax.axis_index("dp")
    sib = me + 1 - 2 * lax.rem(me, 2)
    nx = me + 2 - 4 * lax.rem(me // 2, 2)
    ny = me + 4 - 8 * (me // 4)
    token_count, width = tok_ref.shape
    span = width // CHUNKS
    half = token_count // 2
    own = token_count // dp_count
    hid = w_out.shape[0]
    all_rows = 8 * token_count
    core_rows = 4 * token_count

    loads = [
        pltpu.make_async_copy(gate_hbm, w_in.at[pl.ds(0, hid)], w_sem.at[0]),
        pltpu.make_async_copy(up_hbm, w_in.at[pl.ds(hid, hid)], w_sem.at[1]),
        pltpu.make_async_copy(down_hbm, w_out, w_sem.at[2]),
    ]
    for load in loads:
        load.start()

    barrier = pltpu.get_barrier_semaphore()
    for peer in (sib, nx, ny):
        pl.semaphore_signal(barrier, inc=1, device_id={"expert": peer}, device_id_type=MESH)
    for step in range(1, dp_count):
        pl.semaphore_signal(
            barrier,
            inc=1,
            device_id={"dp": lax.rem(plane + step, dp_count)},
            device_id_type=MESH,
        )

    tok = tok_ref[...].astype(jnp.float32)
    inv_rms = lax.rsqrt(jnp.mean(tok * tok, axis=-1, keepdims=True) + 1e-06)
    for c in range(CHUNKS):
        cols = slice(c * span, (c + 1) * span)
        part = tok_ref[:, cols].astype(jnp.float32) * inv_rms * gain_ref[:, cols]
        rows[c, OWN] = part.astype(jnp.bfloat16)
    dense[OWN] = jnp.zeros(dense.shape[1:], dense.dtype)
    dense[OWN, :, :token_count] = dense_ref[...]

    pl.semaphore_wait(barrier, 3 + dp_count - 1)

    def push(src, dst, send, recv, **where):
        return pltpu.make_async_remote_copy(
            src_ref=src,
            dst_ref=dst,
            send_sem=send,
            recv_sem=recv,
            device_id=where,
            device_id_type=MESH,
        )

    def dense_push(k, src, dst, peer):
        return push(dense.at[src], dense.at[dst], d_send.at[k], d_recv.at[k], expert=peer)

    dense_copies = [
        dense_push(0, OWN, ALONG_X, nx),
        dense_push(1, OWN, ALONG_Y, ny),
        dense_push(2, OWN, SIBLING, sib),
        dense_push(3, ALONG_X, DIAGONAL, ny),
        dense_push(4, ALONG_X, SIBLING + ALONG_X, sib),
        dense_push(5, ALONG_Y, SIBLING + ALONG_Y, sib),
        dense_push(6, DIAGONAL, SIBLING + DIAGONAL, sib),
    ]

    def gather_copies(c):
        def go(k, src, dst, peer, part=None):
            a, b = rows.at[c, src], rows.at[c, dst]
            if part is not None:
                a = rows.at[c, src, pl.ds(part * half, half)]
                b = rows.at[c, dst, pl.ds(part * half, half)]
            return push(a, b, a_send.at[c, k], a_recv.at[c, k], expert=peer)

        return [
            go(0, OWN, ALONG_X, nx),
            go(1, OWN, ALONG_Y, ny),
            go(2, OWN, SIBLING, sib),
            go(3, ALONG_X, DIAGONAL, ny, 0),
            go(4, ALONG_Y, DIAGONAL, nx, 1),
            go(5, ALONG_X, SIBLING + ALONG_X, sib),
            go(6, ALONG_Y, SIBLING + ALONG_Y, sib),
            go(7, DIAGONAL, SIBLING + DIAGONAL, sib),
        ]

    gather = [gather_copies(c) for c in range(CHUNKS)]
    for k in range(3):
        dense_copies[k].start()
    for c in range(CHUNKS):
        for k in range(3):
            gather[c][k].start()

    def forward(c):
        gather[c][0].wait_recv()
        gather[c][3].start()
        gather[c][5].start()
        gather[c][1].wait_recv()
        gather[c][4].start()
        gather[c][6].start()

    def forward_diagonal(c):
        gather[c][3].wait_recv()
        gather[c][4].wait_recv()
        gather[c][7].start()

    def multiply_in(c):
        for k in (2, 5, 6, 7):
            gather[c][k].wait_recv()

        flipped[...] = rows[c].reshape(all_rows, span).T

        @pl.loop(0, 2)
        def _(t):
            w = w_in[pl.ds(pl.multiple_of(t * hid, hid), hid), c * span : (c + 1) * span]
            y = jnp.dot(w, flipped[...], preferred_element_type=jnp.float32)
            if c == 0:
                acc[t] = y
            else:
                acc[t] += y

    forward(0)
    dense_copies[0].wait_recv()
    dense_copies[3].start()
    dense_copies[4].start()
    dense_copies[1].wait_recv()
    dense_copies[5].start()
    forward(1)
    forward_diagonal(0)
    dense_copies[3].wait_recv()
    dense_copies[6].start()
    loads[0].wait()
    loads[1].wait()
    multiply_in(0)
    forward(2)
    forward_diagonal(1)
    multiply_in(1)
    forward(3)
    forward_diagonal(2)
    multiply_in(2)
    forward_diagonal(3)
    for k in (2, 4, 5, 6):
        dense_copies[k].wait_recv()
    multiply_in(3)

    expert_rows = lax.broadcasted_iota(jnp.int32, dense.shape[1:], 0)
    per_expert = hid // local_experts
    for j in range(local_experts):
        scale = jnp.concatenate(
            [
                jnp.sum(
                    jnp.where(expert_rows == me * local_experts + j, dense[p], 0.0),
                    axis=0,
                    keepdims=True,
                )[:, :token_count]
                for p in range(8)
            ],
            axis=1,
        )
        for k in range(j * per_expert, (j + 1) * per_expert, 128):
            g = acc[0, k : k + 128]
            h = g / (1.0 + jnp.exp(-g)) * acc[1, k : k + 128] * scale
            hidden[:, k : k + 128] = h.astype(jnp.bfloat16).T

    def reduce_copies(n):
        def go(k, src, dst, **where):
            return push(src, dst, r_send.at[n, k], r_recv.at[n, k], **where)

        copies = [
            go(0, to_sib.at[n], from_sib.at[n], expert=sib),
            go(1, to_x.at[n], from_x.at[n], expert=nx),
            go(2, to_y.at[n], from_y.at[n], expert=ny),
            go(3, to_y2.at[n], from_y2.at[n], expert=ny),
            go(4, to_x2.at[n], from_x2.at[n], expert=nx),
        ]
        for step in range(1, dp_count):
            peer = lax.rem(plane + step, dp_count)
            copies.append(go(4 + step, to_z.at[n, peer], from_z.at[n, step - 1], dp=peer))
        return copies

    reduce = [reduce_copies(n) for n in range(CHUNKS)]

    def multiply_out(n):
        step = 512

        @pl.loop(0, span // step)
        def _(t):
            w = w_out[:, pl.ds(pl.multiple_of(n * span + t * step, step), step)]
            y = jnp.dot(hidden[...], w, preferred_element_type=jnp.float32)
            cols = pl.ds(pl.multiple_of(t * step, step), step)
            to_sib[n, :, cols] = y[core_rows:].astype(jnp.bfloat16)
            kept[n, :, cols] = y[:core_rows]

        reduce[n][0].start()

    def block(place, part):
        return slice(place * token_count + part * half, place * token_count + (part + 1) * half)

    def pair_sum(n):
        reduce[n][0].wait_recv()

        def total(place, part):
            at = block(place, part)
            return kept[n, at] + from_sib[n, at].astype(jnp.float32)

        to_x[n, :half] = total(ALONG_X, 0).astype(jnp.bfloat16)
        to_x[n, half:] = total(DIAGONAL, 0).astype(jnp.bfloat16)
        reduce[n][1].start()
        to_y[n, :half] = total(ALONG_Y, 1).astype(jnp.bfloat16)
        to_y[n, half:] = total(DIAGONAL, 1).astype(jnp.bfloat16)
        reduce[n][2].start()
        for place, part in ((OWN, 0), (OWN, 1), (ALONG_Y, 0), (ALONG_X, 1)):
            kept[n, block(place, part)] = total(place, part)

    def second_hop(n):
        reduce[n][1].wait_recv()
        to_y2[n] = (
            kept[n, block(ALONG_Y, 0)] + from_x[n, half:].astype(jnp.float32)
        ).astype(jnp.bfloat16)
        reduce[n][3].start()
        reduce[n][2].wait_recv()
        to_x2[n] = (
            kept[n, block(ALONG_X, 1)] + from_y[n, half:].astype(jnp.float32)
        ).astype(jnp.bfloat16)
        reduce[n][4].start()

    def across_planes(n):
        reduce[n][3].wait_recv()
        reduce[n][4].wait_recv()
        first = (
            kept[n, block(OWN, 0)]
            + from_x[n, :half].astype(jnp.float32)
            + from_y2[n].astype(jnp.float32)
        )
        second = (
            kept[n, block(OWN, 1)]
            + from_y[n, :half].astype(jnp.float32)
            + from_x2[n].astype(jnp.float32)
        )
        per_half = half // own
        for i in range(per_half):
            at = slice(i * own, (i + 1) * own)
            summed[n, i] = first[at]
            summed[n, per_half + i] = second[at]
            to_z[n, i] = first[at].astype(jnp.bfloat16)
            to_z[n, per_half + i] = second[at].astype(jnp.bfloat16)
        for step in range(1, dp_count):
            reduce[n][4 + step].start()

    def finish(n):
        result = summed[n, plane]
        for step in range(1, dp_count):
            reduce[n][4 + step].wait_recv()
            result = result + from_z[n, step - 1].astype(jnp.float32)
        out_ref[:, n * span : (n + 1) * span] = result.astype(jnp.bfloat16)

    loads[2].wait()
    multiply_out(0)
    multiply_out(1)
    pair_sum(0)
    multiply_out(2)
    pair_sum(1)
    multiply_out(3)
    pair_sum(2)
    second_hop(0)
    pair_sum(3)
    second_hop(1)
    across_planes(0)
    second_hop(2)
    across_planes(1)
    second_hop(3)
    across_planes(2)
    finish(0)
    across_planes(3)
    finish(1)
    finish(2)
    finish(3)

    for copy in dense_copies:
        copy.wait_send()
    for copies in gather + reduce:
        for copy in copies:
            copy.wait_send()


def fused_body(tokens, norm_gain, expert_ids, route_weights, gate_proj, up_proj, down_proj):
    dp_count = lax.axis_size("dp")
    local_experts, block_hid, width = gate_proj.shape
    experts = local_experts * lax.axis_size("expert")
    token_count = tokens.shape[1]
    hid = local_experts * block_hid
    span = width // CHUNKS
    half = token_count // 2
    own = token_count // dp_count
    core_rows = 4 * token_count

    named = expert_ids[0].T[None] == jnp.arange(experts, dtype=jnp.int32)[:, None, None]
    dense = jnp.sum(jnp.where(named, route_weights[0].T[None], 0.0), axis=1)

    bf16, f32 = jnp.bfloat16, jnp.float32
    vmem = pl.BlockSpec(memory_space=pltpu.VMEM)
    anywhere = pl.BlockSpec(memory_space=pl.ANY)
    dma = pltpu.SemaphoreType.DMA
    mixed = pl.pallas_call(
        functools.partial(fused, dp_count, local_experts),
        out_shape=jax.ShapeDtypeStruct((own, width), bf16),
        in_specs=[vmem] * 3 + [anywhere] * 3,
        out_specs=vmem,
        scratch_shapes=[
            pltpu.VMEM((2 * hid, width), bf16),
            pltpu.VMEM((hid, width), bf16),
            pltpu.VMEM((CHUNKS, 8, token_count, span), bf16),
            pltpu.VMEM((span, 8 * token_count), bf16),
            pltpu.VMEM((8, experts, 128), f32),
            pltpu.VMEM((2, hid, 8 * token_count), f32),
            pltpu.VMEM((8 * token_count, hid), bf16),
            pltpu.VMEM((CHUNKS, core_rows, span), bf16),
            pltpu.VMEM((CHUNKS, core_rows, span), f32),
            pltpu.VMEM((CHUNKS, core_rows, span), bf16),
            pltpu.VMEM((CHUNKS, 2 * half, span), bf16),
            pltpu.VMEM((CHUNKS, 2 * half, span), bf16),
            pltpu.VMEM((CHUNKS, 2 * half, span), bf16),
            pltpu.VMEM((CHUNKS, 2 * half, span), bf16),
            pltpu.VMEM((CHUNKS, half, span), bf16),
            pltpu.VMEM((CHUNKS, half, span), bf16),
            pltpu.VMEM((CHUNKS, half, span), bf16),
            pltpu.VMEM((CHUNKS, half, span), bf16),
            pltpu.VMEM((CHUNKS, dp_count, own, span), f32),
            pltpu.VMEM((CHUNKS, dp_count, own, span), bf16),
            pltpu.VMEM((CHUNKS, dp_count - 1, own, span), bf16),
            dma((3,)),
            dma((7,)),
            dma((7,)),
            dma((CHUNKS, 8)),
            dma((CHUNKS, 8)),
            dma((CHUNKS, 4 + dp_count)),
            dma((CHUNKS, 4 + dp_count)),
        ],
        compiler_params=pltpu.CompilerParams(
            collective_id=0, has_side_effects=True, vmem_limit_bytes=56 * 1024 * 1024
        ),
        cost_estimate=pl.CostEstimate(
            flops=2 * 3 * 8 * token_count * hid * width,
            bytes_accessed=3 * hid * width * 2,
            transcendentals=8 * token_count * hid,
        ),
    )(
        tokens[0],
        norm_gain[None],
        dense,
        gate_proj.reshape(hid, width),
        up_proj.reshape(hid, width),
        down_proj.reshape(hid, width),
    )
    return mixed[None]


def rank_slots(id_table, expert_total):
    flat_ids = id_table.reshape(-1)
    onehot = (flat_ids[:, None] == jnp.arange(expert_total, dtype=jnp.int32)[None, :]).astype(
        jnp.int32
    )
    before = jnp.cumsum(onehot, axis=0) - onehot
    return jnp.sum(before * onehot, axis=1).reshape(id_table.shape)


def body(tokens, norm_gain, expert_ids, route_weights, gate_proj, up_proj, down_proj):
    dp_count = lax.axis_size("dp")
    expert_count = lax.axis_size("expert")
    local_experts = gate_proj.shape[0]
    model_width = tokens.shape[2]
    group_ids = expert_ids[0]
    group_weights = route_weights[0]
    group_size = group_ids.shape[0]
    own_rows = group_size // dp_count
    top_k = group_ids.shape[1]
    experts = local_experts * expert_count
    capacity = dp_count * (group_size * top_k // (experts * dp_count) + 1)
    tok_float = tokens[0].astype(jnp.float32)
    inv_rms = lax.rsqrt(jnp.mean(tok_float * tok_float, axis=-1, keepdims=True) + 1e-06)
    group_rows = (tok_float * inv_rms * norm_gain).astype(jnp.bfloat16)
    slot_rank = rank_slots(group_ids, experts)
    slot_index = group_ids * capacity + slot_rank
    token_order = jnp.broadcast_to(
        jnp.arange(group_size, dtype=jnp.int32)[:, None], (group_size, top_k)
    )
    sources = (
        jnp.full((experts * capacity,), group_size, jnp.int32)
        .at[slot_index.reshape(-1)]
        .set(token_order.reshape(-1))
    )
    padded = jnp.concatenate([group_rows, jnp.zeros((1, model_width), jnp.bfloat16)], axis=0)
    outgoing = jnp.take(padded, sources, axis=0).reshape(
        expert_count, local_experts, capacity, model_width
    )
    incoming = lax.all_to_all(outgoing, "expert", split_axis=0, concat_axis=0, tiled=True)
    gate_act = jnp.einsum("sjmd,jfd->sjmf", incoming, gate_proj, preferred_element_type=jnp.float32)
    up_act = jnp.einsum("sjmd,jfd->sjmf", incoming, up_proj, preferred_element_type=jnp.float32)
    hidden = (jax.nn.silu(gate_act) * up_act).astype(jnp.bfloat16)
    partial_rows = jnp.einsum(
        "sjmf,jfd->sjmd", hidden, down_proj, preferred_element_type=jnp.float32
    ).astype(jnp.bfloat16)
    returned = lax.all_to_all(partial_rows, "expert", split_axis=0, concat_axis=0, tiled=True)
    lookup = jnp.concatenate(
        [
            returned.reshape(experts * capacity, model_width),
            jnp.zeros((1, model_width), jnp.bfloat16),
        ],
        axis=0,
    )
    picked = (
        jnp.take(lookup, slot_index.reshape(-1), axis=0)
        .reshape(own_rows * lax.axis_size("dp"), top_k, model_width)
        .astype(jnp.float32)
    )
    mixed = lax.psum_scatter(
        jnp.sum(picked * group_weights[:, :, None], axis=1).astype(jnp.bfloat16),
        "dp",
        scatter_dimension=0,
        tiled=True,
    )
    return mixed[None]


def solution(mesh):
    placed = (
        P("expert", None, None),
        P(),
        P("expert", None, None),
        P("expert", None, None),
        P("expert", "dp", None),
        P("expert", "dp", None),
        P("expert", "dp", None),
    )
    small = mesh.shape["expert"] == 8 and mesh.shape["dp"] == 4
    return jax.shard_map(
        fused_body if small else body, mesh=mesh, in_specs=placed, out_specs=P("expert", "dp", None), check_vma=False
    )
```

```python
import functools

import jax
import jax.numpy as jnp
from jax import lax
from jax.experimental import pallas as pl
from jax.experimental.pallas import tpu as pltpu
from jax.sharding import PartitionSpec as P

MESH = pl.DeviceIdType.MESH
BATCHES = 2
IN_CHUNKS = 2
OUT_CHUNKS = 2
IN_STEPS = BATCHES * IN_CHUNKS
OUT_STEPS = BATCHES * OUT_CHUNKS
OWN, ALONG_X, ALONG_Y, DIAGONAL, SIBLING = 0, 1, 2, 3, 4


def fused(
    dp_count,
    local_experts,
    tok_ref,
    gain_ref,
    dense_ref,
    gate_hbm,
    up_hbm,
    down_hbm,
    out_ref,
    w_in,
    w_out,
    rows,
    flipped,
    dense,
    acc,
    hidden,
    to_sib,
    kept,
    from_sib,
    to_x,
    to_y,
    from_x,
    from_y,
    to_x2,
    to_y2,
    from_x2,
    from_y2,
    summed,
    to_z,
    from_z,
    result,
    w_sem,
    d_send,
    d_recv,
    a_send,
    a_recv,
    r_send,
    r_recv,
):
    me = lax.axis_index("expert")
    plane = lax.axis_index("dp")
    sib = me + 1 - 2 * lax.rem(me, 2)
    nx = me + 2 - 4 * lax.rem(me // 2, 2)
    ny = me + 4 - 8 * (me // 4)
    token_count, width = tok_ref.shape
    in_span = width // IN_CHUNKS
    out_span = width // OUT_CHUNKS
    batch = token_count // BATCHES
    half = batch // 2
    own = token_count // dp_count
    piece = own // BATCHES
    hid = w_out.shape[0]
    all_rows = 8 * batch
    core_rows = 4 * batch

    loads = [
        pltpu.make_async_copy(gate_hbm, w_in.at[pl.ds(0, hid)], w_sem.at[0]),
        pltpu.make_async_copy(up_hbm, w_in.at[pl.ds(hid, hid)], w_sem.at[1]),
        pltpu.make_async_copy(down_hbm, w_out, w_sem.at[2]),
    ]
    for load in loads:
        load.start()

    barrier = pltpu.get_barrier_semaphore()
    for peer in (sib, nx, ny):
        pl.semaphore_signal(barrier, inc=1, device_id={"expert": peer}, device_id_type=MESH)
    for step in range(1, dp_count):
        pl.semaphore_signal(
            barrier,
            inc=1,
            device_id={"dp": lax.rem(plane + step, dp_count)},
            device_id_type=MESH,
        )

    tok = tok_ref[...].astype(jnp.float32)
    inv_rms = lax.rsqrt(jnp.mean(tok * tok, axis=-1, keepdims=True) + 1e-06)
    for c in range(IN_CHUNKS):
        cols = slice(c * in_span, (c + 1) * in_span)
        part = tok_ref[:, cols].astype(jnp.float32) * inv_rms * gain_ref[:, cols]
        for b in range(BATCHES):
            picked = [
                part[z * own + b * piece : z * own + (b + 1) * piece] for z in range(dp_count)
            ]
            rows[b * IN_CHUNKS + c, OWN] = jnp.concatenate(picked, axis=0).astype(jnp.bfloat16)
    dense[OWN] = jnp.zeros(dense.shape[1:], dense.dtype)
    dense[OWN, :, :token_count] = dense_ref[...]

    pl.semaphore_wait(barrier, 3 + dp_count - 1)

    def push(src, dst, send, recv, **where):
        return pltpu.make_async_remote_copy(
            src_ref=src,
            dst_ref=dst,
            send_sem=send,
            recv_sem=recv,
            device_id=where,
            device_id_type=MESH,
        )

    def dense_push(k, src, dst, peer):
        return push(dense.at[src], dense.at[dst], d_send.at[k], d_recv.at[k], expert=peer)

    dense_copies = [
        dense_push(0, OWN, ALONG_X, nx),
        dense_push(1, OWN, ALONG_Y, ny),
        dense_push(2, OWN, SIBLING, sib),
        dense_push(3, ALONG_X, DIAGONAL, ny),
        dense_push(4, ALONG_X, SIBLING + ALONG_X, sib),
        dense_push(5, ALONG_Y, SIBLING + ALONG_Y, sib),
        dense_push(6, DIAGONAL, SIBLING + DIAGONAL, sib),
    ]

    def gather_copies(c):
        def go(k, src, dst, peer, part=None):
            a, b = rows.at[c, src], rows.at[c, dst]
            if part is not None:
                a = rows.at[c, src, pl.ds(part * half, half)]
                b = rows.at[c, dst, pl.ds(part * half, half)]
            return push(a, b, a_send.at[c, k], a_recv.at[c, k], expert=peer)

        return [
            go(0, OWN, ALONG_X, nx),
            go(1, OWN, ALONG_Y, ny),
            go(2, OWN, SIBLING, sib),
            go(3, ALONG_X, DIAGONAL, ny, 0),
            go(4, ALONG_Y, DIAGONAL, nx, 1),
            go(5, ALONG_X, SIBLING + ALONG_X, sib),
            go(6, ALONG_Y, SIBLING + ALONG_Y, sib),
            go(7, DIAGONAL, SIBLING + DIAGONAL, sib),
        ]

    gather = [gather_copies(s) for s in range(IN_STEPS)]
    for k in range(3):
        dense_copies[k].start()
    for s in range(IN_STEPS):
        for k in range(3):
            gather[s][k].start()

    def forward(c):
        gather[c][0].wait_recv()
        gather[c][3].start()
        gather[c][5].start()
        gather[c][1].wait_recv()
        gather[c][4].start()
        gather[c][6].start()

    def forward_diagonal(c):
        gather[c][3].wait_recv()
        gather[c][4].wait_recv()
        gather[c][7].start()

    def multiply_in(s):
        c = s % IN_CHUNKS
        for k in (2, 5, 6, 7):
            gather[s][k].wait_recv()
        flipped[...] = rows[s].reshape(all_rows, in_span).T

        @pl.loop(0, 2)
        def _(t):
            w = w_in[
                pl.ds(pl.multiple_of(t * hid, hid), hid), c * in_span : (c + 1) * in_span
            ]
            y = jnp.dot(w, flipped[...], preferred_element_type=jnp.float32)
            if c == 0:
                acc[t] = y
            else:
                acc[t] += y

    expert_rows = lax.broadcasted_iota(jnp.int32, dense.shape[1:], 0)
    per_expert = hid // local_experts

    def activate(b):
        for j in range(local_experts):
            scale = jnp.concatenate(
                [
                    jnp.sum(
                        jnp.where(expert_rows == me * local_experts + j, dense[p], 0.0),
                        axis=0,
                        keepdims=True,
                    )[:, b * batch : (b + 1) * batch]
                    for p in range(8)
                ],
                axis=1,
            )
            for k in range(j * per_expert, (j + 1) * per_expert, 128):
                g = acc[0, k : k + 128]
                h = g / (1.0 + jnp.exp(-g)) * acc[1, k : k + 128] * scale
                hidden[:, k : k + 128] = h.astype(jnp.bfloat16).T

    def reduce_copies(n):
        def go(k, src, dst, **where):
            return push(src, dst, r_send.at[n, k], r_recv.at[n, k], **where)

        copies = [
            go(0, to_sib.at[n], from_sib.at[n], expert=sib),
            go(1, to_x.at[n], from_x.at[n], expert=nx),
            go(2, to_y.at[n], from_y.at[n], expert=ny),
            go(3, to_y2.at[n], from_y2.at[n], expert=ny),
            go(4, to_x2.at[n], from_x2.at[n], expert=nx),
        ]
        for step in range(1, dp_count):
            peer = lax.rem(plane + step, dp_count)
            copies.append(go(4 + step, to_z.at[n, peer], from_z.at[n, step - 1], dp=peer))
        return copies

    reduce = [reduce_copies(n) for n in range(OUT_STEPS)]

    def multiply_out(n):
        step = 512

        @pl.loop(0, out_span // step)
        def _(t):
            w = w_out[:, pl.ds(pl.multiple_of(n % OUT_CHUNKS * out_span + t * step, step), step)]
            y = jnp.dot(hidden[...], w, preferred_element_type=jnp.float32)
            cols = pl.ds(pl.multiple_of(t * step, step), step)
            to_sib[n, :, cols] = y[core_rows:].astype(jnp.bfloat16)
            kept[n, :, cols] = y[:core_rows]

        reduce[n][0].start()

    def block(place, part):
        return slice(place * batch + part * half, place * batch + (part + 1) * half)

    def pair_sum(n):
        reduce[n][0].wait_recv()

        def total(place, part):
            at = block(place, part)
            return kept[n, at] + from_sib[n, at].astype(jnp.float32)

        to_x[n, :half] = total(ALONG_X, 0).astype(jnp.bfloat16)
        to_x[n, half:] = total(DIAGONAL, 0).astype(jnp.bfloat16)
        reduce[n][1].start()
        to_y[n, :half] = total(ALONG_Y, 1).astype(jnp.bfloat16)
        to_y[n, half:] = total(DIAGONAL, 1).astype(jnp.bfloat16)
        reduce[n][2].start()
        for place, part in ((OWN, 0), (OWN, 1), (ALONG_Y, 0), (ALONG_X, 1)):
            kept[n, block(place, part)] = total(place, part)

    def second_hop(n):
        reduce[n][1].wait_recv()
        to_y2[n] = (
            kept[n, block(ALONG_Y, 0)] + from_x[n, half:].astype(jnp.float32)
        ).astype(jnp.bfloat16)
        reduce[n][3].start()
        reduce[n][2].wait_recv()
        to_x2[n] = (
            kept[n, block(ALONG_X, 1)] + from_y[n, half:].astype(jnp.float32)
        ).astype(jnp.bfloat16)
        reduce[n][4].start()

    def across_planes(n):
        reduce[n][3].wait_recv()
        reduce[n][4].wait_recv()
        first = (
            kept[n, block(OWN, 0)]
            + from_x[n, :half].astype(jnp.float32)
            + from_y2[n].astype(jnp.float32)
        )
        second = (
            kept[n, block(OWN, 1)]
            + from_y[n, :half].astype(jnp.float32)
            + from_x2[n].astype(jnp.float32)
        )
        per_half = half // piece
        for i in range(dp_count):
            source = first if i < per_half else second
            at = i % per_half * piece
            rows_i = source[at : at + piece]
            folded = jnp.concatenate(
                [rows_i[:, f * fold : (f + 1) * fold] for f in range(BATCHES)], axis=0
            )
            summed[n, i] = folded
            to_z[n, i] = folded.astype(jnp.bfloat16)
        for step in range(1, dp_count):
            reduce[n][4 + step].start()

    fold = out_span // BATCHES

    def finish(n):
        total = summed[n, plane]
        for step in range(1, dp_count):
            reduce[n][4 + step].wait_recv()
            total = total + from_z[n, step - 1].astype(jnp.float32)
        b, c = n // OUT_CHUNKS, n % OUT_CHUNKS
        for f in range(BATCHES):
            at = c * out_span + f * fold
            result[b * piece : (b + 1) * piece, at : at + fold] = total[
                f * piece : (f + 1) * piece
            ]

    forward(0)
    dense_copies[0].wait_recv()
    dense_copies[3].start()
    dense_copies[4].start()
    dense_copies[1].wait_recv()
    dense_copies[5].start()
    forward(1)
    forward_diagonal(0)
    dense_copies[3].wait_recv()
    dense_copies[6].start()
    loads[0].wait()
    loads[1].wait()
    multiply_in(0)
    forward(2)
    forward_diagonal(1)
    multiply_in(1)
    for k in (2, 4, 5, 6):
        dense_copies[k].wait_recv()
    activate(0)
    loads[2].wait()
    multiply_out(0)
    multiply_out(1)
    forward_diagonal(2)
    pair_sum(0)
    forward(3)
    multiply_in(2)
    pair_sum(1)
    forward_diagonal(3)
    multiply_in(3)
    second_hop(0)
    activate(1)
    multiply_out(2)
    second_hop(1)
    multiply_out(3)
    pair_sum(2)
    across_planes(0)
    pair_sum(3)
    across_planes(1)
    second_hop(2)
    finish(0)
    second_hop(3)
    finish(1)
    across_planes(2)
    across_planes(3)
    finish(2)
    finish(3)
    out_ref[...] = result[...].astype(jnp.bfloat16)

    for copy in dense_copies:
        copy.wait_send()
    for copies in gather + reduce:
        for copy in copies:
            copy.wait_send()


def fused_body(tokens, norm_gain, expert_ids, route_weights, gate_proj, up_proj, down_proj):
    dp_count = lax.axis_size("dp")
    local_experts, block_hid, width = gate_proj.shape
    experts = local_experts * lax.axis_size("expert")
    token_count = tokens.shape[1]
    hid = local_experts * block_hid
    in_span = width // IN_CHUNKS
    out_span = width // OUT_CHUNKS
    batch = token_count // BATCHES
    half = batch // 2
    own = token_count // dp_count
    core_rows = 4 * batch

    def regroup(table):
        pieces = table.reshape(dp_count, BATCHES, own // BATCHES, table.shape[1])
        return pieces.swapaxes(0, 1).reshape(table.shape).T[None]

    named = regroup(expert_ids[0]) == jnp.arange(experts, dtype=jnp.int32)[:, None, None]
    dense = jnp.sum(jnp.where(named, regroup(route_weights[0]), 0.0), axis=1)

    bf16, f32 = jnp.bfloat16, jnp.float32
    vmem = pl.BlockSpec(memory_space=pltpu.VMEM)
    anywhere = pl.BlockSpec(memory_space=pl.ANY)
    dma = pltpu.SemaphoreType.DMA
    mixed = pl.pallas_call(
        functools.partial(fused, dp_count, local_experts),
        out_shape=jax.ShapeDtypeStruct((own, width), bf16),
        in_specs=[vmem] * 3 + [anywhere] * 3,
        out_specs=vmem,
        scratch_shapes=[
            pltpu.VMEM((2 * hid, width), bf16),
            pltpu.VMEM((hid, width), bf16),
            pltpu.VMEM((IN_STEPS, 8, batch, in_span), bf16),
            pltpu.VMEM((in_span, 8 * batch), bf16),
            pltpu.VMEM((8, experts, 128), f32),
            pltpu.VMEM((2, hid, 8 * batch), f32),
            pltpu.VMEM((8 * batch, hid), bf16),
            pltpu.VMEM((OUT_STEPS, core_rows, out_span), bf16),
            pltpu.VMEM((OUT_STEPS, core_rows, out_span), f32),
            pltpu.VMEM((OUT_STEPS, core_rows, out_span), bf16),
            pltpu.VMEM((OUT_STEPS, 2 * half, out_span), bf16),
            pltpu.VMEM((OUT_STEPS, 2 * half, out_span), bf16),
            pltpu.VMEM((OUT_STEPS, 2 * half, out_span), bf16),
            pltpu.VMEM((OUT_STEPS, 2 * half, out_span), bf16),
            pltpu.VMEM((OUT_STEPS, half, out_span), bf16),
            pltpu.VMEM((OUT_STEPS, half, out_span), bf16),
            pltpu.VMEM((OUT_STEPS, half, out_span), bf16),
            pltpu.VMEM((OUT_STEPS, half, out_span), bf16),
            pltpu.VMEM((OUT_STEPS, dp_count, own, out_span // BATCHES), f32),
            pltpu.VMEM((OUT_STEPS, dp_count, own, out_span // BATCHES), bf16),
            pltpu.VMEM((OUT_STEPS, dp_count - 1, own, out_span // BATCHES), bf16),
            pltpu.VMEM((own, width), f32),
            dma((3,)),
            dma((7,)),
            dma((7,)),
            dma((IN_STEPS, 8)),
            dma((IN_STEPS, 8)),
            dma((OUT_STEPS, 4 + dp_count)),
            dma((OUT_STEPS, 4 + dp_count)),
        ],
        compiler_params=pltpu.CompilerParams(
            collective_id=0, has_side_effects=True, vmem_limit_bytes=56 * 1024 * 1024
        ),
        cost_estimate=pl.CostEstimate(
            flops=2 * 3 * 8 * token_count * hid * width,
            bytes_accessed=3 * hid * width * 2,
            transcendentals=8 * token_count * hid,
        ),
    )(
        tokens[0],
        norm_gain[None],
        dense,
        gate_proj.reshape(hid, width),
        up_proj.reshape(hid, width),
        down_proj.reshape(hid, width),
    )
    return mixed[None]


def rank_slots(id_table, expert_total):
    flat_ids = id_table.reshape(-1)
    onehot = (flat_ids[:, None] == jnp.arange(expert_total, dtype=jnp.int32)[None, :]).astype(
        jnp.int32
    )
    before = jnp.cumsum(onehot, axis=0) - onehot
    return jnp.sum(before * onehot, axis=1).reshape(id_table.shape)


def body(tokens, norm_gain, expert_ids, route_weights, gate_proj, up_proj, down_proj):
    dp_count = lax.axis_size("dp")
    expert_count = lax.axis_size("expert")
    local_experts = gate_proj.shape[0]
    model_width = tokens.shape[2]
    group_ids = expert_ids[0]
    group_weights = route_weights[0]
    group_size = group_ids.shape[0]
    own_rows = group_size // dp_count
    top_k = group_ids.shape[1]
    experts = local_experts * expert_count
    capacity = dp_count * (group_size * top_k // (experts * dp_count) + 1)
    tok_float = tokens[0].astype(jnp.float32)
    inv_rms = lax.rsqrt(jnp.mean(tok_float * tok_float, axis=-1, keepdims=True) + 1e-06)
    group_rows = (tok_float * inv_rms * norm_gain).astype(jnp.bfloat16)
    slot_rank = rank_slots(group_ids, experts)
    slot_index = group_ids * capacity + slot_rank
    token_order = jnp.broadcast_to(
        jnp.arange(group_size, dtype=jnp.int32)[:, None], (group_size, top_k)
    )
    sources = (
        jnp.full((experts * capacity,), group_size, jnp.int32)
        .at[slot_index.reshape(-1)]
        .set(token_order.reshape(-1))
    )
    padded = jnp.concatenate([group_rows, jnp.zeros((1, model_width), jnp.bfloat16)], axis=0)
    outgoing = jnp.take(padded, sources, axis=0).reshape(
        expert_count, local_experts, capacity, model_width
    )
    incoming = lax.all_to_all(outgoing, "expert", split_axis=0, concat_axis=0, tiled=True)
    gate_act = jnp.einsum("sjmd,jfd->sjmf", incoming, gate_proj, preferred_element_type=jnp.float32)
    up_act = jnp.einsum("sjmd,jfd->sjmf", incoming, up_proj, preferred_element_type=jnp.float32)
    hidden = (jax.nn.silu(gate_act) * up_act).astype(jnp.bfloat16)
    partial_rows = jnp.einsum(
        "sjmf,jfd->sjmd", hidden, down_proj, preferred_element_type=jnp.float32
    ).astype(jnp.bfloat16)
    returned = lax.all_to_all(partial_rows, "expert", split_axis=0, concat_axis=0, tiled=True)
    lookup = jnp.concatenate(
        [
            returned.reshape(experts * capacity, model_width),
            jnp.zeros((1, model_width), jnp.bfloat16),
        ],
        axis=0,
    )
    picked = (
        jnp.take(lookup, slot_index.reshape(-1), axis=0)
        .reshape(own_rows * lax.axis_size("dp"), top_k, model_width)
        .astype(jnp.float32)
    )
    mixed = lax.psum_scatter(
        jnp.sum(picked * group_weights[:, :, None], axis=1).astype(jnp.bfloat16),
        "dp",
        scatter_dimension=0,
        tiled=True,
    )
    return mixed[None]


def solution(mesh):
    placed = (
        P("expert", None, None),
        P(),
        P("expert", None, None),
        P("expert", None, None),
        P("expert", "dp", None),
        P("expert", "dp", None),
        P("expert", "dp", None),
    )
    small = mesh.shape["expert"] == 8 and mesh.shape["dp"] == 4
    return jax.shard_map(
        fused_body if small else body, mesh=mesh, in_specs=placed, out_specs=P("expert", "dp", None), check_vma=False
    )
```

```python
import functools

import jax
import jax.numpy as jnp
from jax import lax
from jax.experimental import pallas as pl
from jax.experimental.pallas import tpu as pltpu
from jax.sharding import PartitionSpec as P

MESH = pl.DeviceIdType.MESH
BATCHES = 2
IN_CHUNKS = 2
OUT_CHUNKS = 4
IN_STEPS = BATCHES * IN_CHUNKS
OUT_STEPS = BATCHES * OUT_CHUNKS
OWN, ALONG_X, ALONG_Y, DIAGONAL, SIBLING = 0, 1, 2, 3, 4


def fused(
    dp_count,
    local_experts,
    tok_ref,
    gain_ref,
    dense_ref,
    gate_hbm,
    up_hbm,
    down_hbm,
    out_ref,
    w_in,
    w_out,
    rows,
    flipped,
    dense,
    acc,
    hidden,
    to_sib,
    kept,
    from_sib,
    to_x,
    to_y,
    from_x,
    from_y,
    to_x2,
    to_y2,
    from_x2,
    from_y2,
    summed,
    to_z,
    from_z,
    result,
    w_sem,
    d_send,
    d_recv,
    a_send,
    a_recv,
    r_send,
    r_recv,
):
    me = lax.axis_index("expert")
    plane = lax.axis_index("dp")
    sib = me + 1 - 2 * lax.rem(me, 2)
    nx = me + 2 - 4 * lax.rem(me // 2, 2)
    ny = me + 4 - 8 * (me // 4)
    token_count, width = tok_ref.shape
    in_span = width // IN_CHUNKS
    out_span = width // OUT_CHUNKS
    batch = token_count // BATCHES
    half = batch // 2
    own = token_count // dp_count
    piece = own // BATCHES
    hid = w_out.shape[0]
    all_rows = 8 * batch
    core_rows = 4 * batch

    loads = [
        pltpu.make_async_copy(gate_hbm, w_in.at[pl.ds(0, hid)], w_sem.at[0]),
        pltpu.make_async_copy(up_hbm, w_in.at[pl.ds(hid, hid)], w_sem.at[1]),
        pltpu.make_async_copy(down_hbm, w_out, w_sem.at[2]),
    ]
    for load in loads:
        load.start()

    barrier = pltpu.get_barrier_semaphore()
    for peer in (sib, nx, ny):
        pl.semaphore_signal(barrier, inc=1, device_id={"expert": peer}, device_id_type=MESH)
    for step in range(1, dp_count):
        pl.semaphore_signal(
            barrier,
            inc=1,
            device_id={"dp": lax.rem(plane + step, dp_count)},
            device_id_type=MESH,
        )

    tok = tok_ref[...].astype(jnp.float32)
    inv_rms = lax.rsqrt(jnp.mean(tok * tok, axis=-1, keepdims=True) + 1e-06)
    for c in range(IN_CHUNKS):
        cols = slice(c * in_span, (c + 1) * in_span)
        part = tok_ref[:, cols].astype(jnp.float32) * inv_rms * gain_ref[:, cols]
        for b in range(BATCHES):
            picked = [
                part[z * own + b * piece : z * own + (b + 1) * piece] for z in range(dp_count)
            ]
            rows[b * IN_CHUNKS + c, OWN] = jnp.concatenate(picked, axis=0).astype(jnp.bfloat16)
    dense[OWN] = jnp.zeros(dense.shape[1:], dense.dtype)
    dense[OWN, :, :token_count] = dense_ref[...]

    pl.semaphore_wait(barrier, 3 + dp_count - 1)

    def push(src, dst, send, recv, **where):
        return pltpu.make_async_remote_copy(
            src_ref=src,
            dst_ref=dst,
            send_sem=send,
            recv_sem=recv,
            device_id=where,
            device_id_type=MESH,
        )

    def dense_push(k, src, dst, peer):
        return push(dense.at[src], dense.at[dst], d_send.at[k], d_recv.at[k], expert=peer)

    dense_copies = [
        dense_push(0, OWN, ALONG_X, nx),
        dense_push(1, OWN, ALONG_Y, ny),
        dense_push(2, OWN, SIBLING, sib),
        dense_push(3, ALONG_X, DIAGONAL, ny),
        dense_push(4, ALONG_X, SIBLING + ALONG_X, sib),
        dense_push(5, ALONG_Y, SIBLING + ALONG_Y, sib),
        dense_push(6, DIAGONAL, SIBLING + DIAGONAL, sib),
    ]

    def gather_copies(c):
        def go(k, src, dst, peer, part=None):
            a, b = rows.at[c, src], rows.at[c, dst]
            if part is not None:
                a = rows.at[c, src, pl.ds(part * half, half)]
                b = rows.at[c, dst, pl.ds(part * half, half)]
            return push(a, b, a_send.at[c, k], a_recv.at[c, k], expert=peer)

        return [
            go(0, OWN, ALONG_X, nx),
            go(1, OWN, ALONG_Y, ny),
            go(2, OWN, SIBLING, sib),
            go(3, ALONG_X, DIAGONAL, ny, 0),
            go(4, ALONG_Y, DIAGONAL, nx, 1),
            go(5, ALONG_X, SIBLING + ALONG_X, sib),
            go(6, ALONG_Y, SIBLING + ALONG_Y, sib),
            go(7, DIAGONAL, SIBLING + DIAGONAL, sib),
        ]

    gather = [gather_copies(s) for s in range(IN_STEPS)]
    for k in range(3):
        dense_copies[k].start()

    def share(s):
        for k in range(3):
            gather[s][k].start()

    share(0)
    share(1)

    def forward(c):
        gather[c][0].wait_recv()
        gather[c][3].start()
        gather[c][5].start()
        gather[c][1].wait_recv()
        gather[c][4].start()
        gather[c][6].start()

    def forward_diagonal(c):
        gather[c][3].wait_recv()
        gather[c][4].wait_recv()
        gather[c][7].start()

    def multiply_in(s):
        c = s % IN_CHUNKS
        for k in (2, 5, 6, 7):
            gather[s][k].wait_recv()
        flipped[...] = rows[s].reshape(all_rows, in_span).T

        @pl.loop(0, 2)
        def _(t):
            w = w_in[
                pl.ds(pl.multiple_of(t * hid, hid), hid), c * in_span : (c + 1) * in_span
            ]
            y = jnp.dot(w, flipped[...], preferred_element_type=jnp.float32)
            if c == 0:
                acc[t] = y
            else:
                acc[t] += y

    expert_rows = lax.broadcasted_iota(jnp.int32, dense.shape[1:], 0)
    per_expert = hid // local_experts

    def activate(b):
        for j in range(local_experts):
            scale = jnp.concatenate(
                [
                    jnp.sum(
                        jnp.where(expert_rows == me * local_experts + j, dense[p], 0.0),
                        axis=0,
                        keepdims=True,
                    )[:, b * batch : (b + 1) * batch]
                    for p in range(8)
                ],
                axis=1,
            )
            for k in range(j * per_expert, (j + 1) * per_expert, 128):
                g = acc[0, k : k + 128]
                h = g / (1.0 + jnp.exp(-g)) * acc[1, k : k + 128] * scale
                hidden[:, k : k + 128] = h.astype(jnp.bfloat16).T

    def reduce_copies(n):
        def go(k, src, dst, **where):
            return push(src, dst, r_send.at[n, k], r_recv.at[n, k], **where)

        copies = [
            go(0, to_sib.at[n], from_sib.at[n], expert=sib),
            go(1, to_x.at[n], from_x.at[n], expert=nx),
            go(2, to_y.at[n], from_y.at[n], expert=ny),
            go(3, to_y2.at[n], from_y2.at[n], expert=ny),
            go(4, to_x2.at[n], from_x2.at[n], expert=nx),
        ]
        for step in range(1, dp_count):
            peer = lax.rem(plane + step, dp_count)
            copies.append(go(4 + step, to_z.at[n, peer], from_z.at[n, step - 1], dp=peer))
        return copies

    reduce = [reduce_copies(n) for n in range(OUT_STEPS)]

    def multiply_out(n):
        step = 512

        @pl.loop(0, out_span // step)
        def _(t):
            w = w_out[:, pl.ds(pl.multiple_of(n % OUT_CHUNKS * out_span + t * step, step), step)]
            y = jnp.dot(hidden[...], w, preferred_element_type=jnp.float32)
            cols = pl.ds(pl.multiple_of(t * step, step), step)
            to_sib[n, :, cols] = y[core_rows:].astype(jnp.bfloat16)
            kept[n, :, cols] = y[:core_rows]

        reduce[n][0].start()

    def block(place, part):
        return slice(place * batch + part * half, place * batch + (part + 1) * half)

    def pair_sum(n):
        reduce[n][0].wait_recv()

        def total(place, part):
            at = block(place, part)
            return kept[n, at] + from_sib[n, at].astype(jnp.float32)

        to_x[n, :half] = total(ALONG_X, 0).astype(jnp.bfloat16)
        to_x[n, half:] = total(DIAGONAL, 0).astype(jnp.bfloat16)
        reduce[n][1].start()
        to_y[n, :half] = total(ALONG_Y, 1).astype(jnp.bfloat16)
        to_y[n, half:] = total(DIAGONAL, 1).astype(jnp.bfloat16)
        reduce[n][2].start()
        for place, part in ((OWN, 0), (OWN, 1), (ALONG_Y, 0), (ALONG_X, 1)):
            kept[n, block(place, part)] = total(place, part)

    def second_hop(n):
        reduce[n][1].wait_recv()
        to_y2[n] = (
            kept[n, block(ALONG_Y, 0)] + from_x[n, half:].astype(jnp.float32)
        ).astype(jnp.bfloat16)
        reduce[n][3].start()
        reduce[n][2].wait_recv()
        to_x2[n] = (
            kept[n, block(ALONG_X, 1)] + from_y[n, half:].astype(jnp.float32)
        ).astype(jnp.bfloat16)
        reduce[n][4].start()

    def across_planes(n):
        reduce[n][3].wait_recv()
        reduce[n][4].wait_recv()
        first = (
            kept[n, block(OWN, 0)]
            + from_x[n, :half].astype(jnp.float32)
            + from_y2[n].astype(jnp.float32)
        )
        second = (
            kept[n, block(OWN, 1)]
            + from_y[n, :half].astype(jnp.float32)
            + from_x2[n].astype(jnp.float32)
        )
        per_half = half // piece
        for i in range(dp_count):
            source = first if i < per_half else second
            at = i % per_half * piece
            rows_i = source[at : at + piece]
            folded = jnp.concatenate(
                [rows_i[:, f * fold : (f + 1) * fold] for f in range(BATCHES)], axis=0
            )
            summed[n, i] = folded
            to_z[n, i] = folded.astype(jnp.bfloat16)
        for step in range(1, dp_count):
            reduce[n][4 + step].start()

    fold = out_span // BATCHES

    def finish(n):
        total = summed[n, plane]
        for step in range(1, dp_count):
            reduce[n][4 + step].wait_recv()
            total = total + from_z[n, step - 1].astype(jnp.float32)
        b, c = n // OUT_CHUNKS, n % OUT_CHUNKS
        for f in range(BATCHES):
            at = c * out_span + f * fold
            result[b * piece : (b + 1) * piece, at : at + fold] = total[
                f * piece : (f + 1) * piece
            ]

    forward(0)
    share(2)
    dense_copies[0].wait_recv()
    dense_copies[3].start()
    dense_copies[4].start()
    dense_copies[1].wait_recv()
    dense_copies[5].start()
    forward(1)
    share(3)
    forward_diagonal(0)
    dense_copies[3].wait_recv()
    dense_copies[6].start()
    loads[0].wait()
    loads[1].wait()
    multiply_in(0)
    forward_diagonal(1)
    forward(2)
    multiply_in(1)
    for k in (2, 4, 5, 6):
        dense_copies[k].wait_recv()
    activate(0)
    loads[2].wait()
    multiply_out(0)
    multiply_out(1)
    forward(3)
    multiply_out(2)
    pair_sum(0)
    multiply_out(3)
    pair_sum(1)
    forward_diagonal(2)
    multiply_in(2)
    pair_sum(2)
    pair_sum(3)
    forward_diagonal(3)
    multiply_in(3)
    second_hop(0)
    second_hop(1)
    activate(1)
    multiply_out(4)
    second_hop(2)
    multiply_out(5)
    pair_sum(4)
    second_hop(3)
    multiply_out(6)
    pair_sum(5)
    across_planes(0)
    multiply_out(7)
    pair_sum(6)
    across_planes(1)
    pair_sum(7)
    across_planes(2)
    across_planes(3)
    second_hop(4)
    finish(0)
    second_hop(5)
    finish(1)
    across_planes(4)
    second_hop(6)
    finish(2)
    across_planes(5)
    second_hop(7)
    finish(3)
    across_planes(6)
    finish(4)
    across_planes(7)
    finish(5)
    finish(6)
    finish(7)
    out_ref[...] = result[...].astype(jnp.bfloat16)

    for copy in dense_copies:
        copy.wait_send()
    for copies in gather + reduce:
        for copy in copies:
            copy.wait_send()


def fused_body(tokens, norm_gain, expert_ids, route_weights, gate_proj, up_proj, down_proj):
    dp_count = lax.axis_size("dp")
    local_experts, block_hid, width = gate_proj.shape
    experts = local_experts * lax.axis_size("expert")
    token_count = tokens.shape[1]
    hid = local_experts * block_hid
    in_span = width // IN_CHUNKS
    out_span = width // OUT_CHUNKS
    batch = token_count // BATCHES
    half = batch // 2
    own = token_count // dp_count
    core_rows = 4 * batch

    def regroup(table):
        pieces = table.reshape(dp_count, BATCHES, own // BATCHES, table.shape[1])
        return pieces.swapaxes(0, 1).reshape(table.shape).T[None]

    named = regroup(expert_ids[0]) == jnp.arange(experts, dtype=jnp.int32)[:, None, None]
    dense = jnp.sum(jnp.where(named, regroup(route_weights[0]), 0.0), axis=1)

    bf16, f32 = jnp.bfloat16, jnp.float32
    vmem = pl.BlockSpec(memory_space=pltpu.VMEM)
    anywhere = pl.BlockSpec(memory_space=pl.ANY)
    dma = pltpu.SemaphoreType.DMA
    mixed = pl.pallas_call(
        functools.partial(fused, dp_count, local_experts),
        out_shape=jax.ShapeDtypeStruct((own, width), bf16),
        in_specs=[vmem] * 3 + [anywhere] * 3,
        out_specs=vmem,
        scratch_shapes=[
            pltpu.VMEM((2 * hid, width), bf16),
            pltpu.VMEM((hid, width), bf16),
            pltpu.VMEM((IN_STEPS, 8, batch, in_span), bf16),
            pltpu.VMEM((in_span, 8 * batch), bf16),
            pltpu.VMEM((8, experts, 128), f32),
            pltpu.VMEM((2, hid, 8 * batch), f32),
            pltpu.VMEM((8 * batch, hid), bf16),
            pltpu.VMEM((OUT_STEPS, core_rows, out_span), bf16),
            pltpu.VMEM((OUT_STEPS, core_rows, out_span), f32),
            pltpu.VMEM((OUT_STEPS, core_rows, out_span), bf16),
            pltpu.VMEM((OUT_STEPS, 2 * half, out_span), bf16),
            pltpu.VMEM((OUT_STEPS, 2 * half, out_span), bf16),
            pltpu.VMEM((OUT_STEPS, 2 * half, out_span), bf16),
            pltpu.VMEM((OUT_STEPS, 2 * half, out_span), bf16),
            pltpu.VMEM((OUT_STEPS, half, out_span), bf16),
            pltpu.VMEM((OUT_STEPS, half, out_span), bf16),
            pltpu.VMEM((OUT_STEPS, half, out_span), bf16),
            pltpu.VMEM((OUT_STEPS, half, out_span), bf16),
            pltpu.VMEM((OUT_STEPS, dp_count, own, out_span // BATCHES), f32),
            pltpu.VMEM((OUT_STEPS, dp_count, own, out_span // BATCHES), bf16),
            pltpu.VMEM((OUT_STEPS, dp_count - 1, own, out_span // BATCHES), bf16),
            pltpu.VMEM((own, width), f32),
            dma((3,)),
            dma((7,)),
            dma((7,)),
            dma((IN_STEPS, 8)),
            dma((IN_STEPS, 8)),
            dma((OUT_STEPS, 4 + dp_count)),
            dma((OUT_STEPS, 4 + dp_count)),
        ],
        compiler_params=pltpu.CompilerParams(
            collective_id=0, has_side_effects=True, vmem_limit_bytes=56 * 1024 * 1024
        ),
        cost_estimate=pl.CostEstimate(
            flops=2 * 3 * 8 * token_count * hid * width,
            bytes_accessed=3 * hid * width * 2,
            transcendentals=8 * token_count * hid,
        ),
    )(
        tokens[0],
        norm_gain[None],
        dense,
        gate_proj.reshape(hid, width),
        up_proj.reshape(hid, width),
        down_proj.reshape(hid, width),
    )
    return mixed[None]


def rank_slots(id_table, expert_total):
    flat_ids = id_table.reshape(-1)
    onehot = (flat_ids[:, None] == jnp.arange(expert_total, dtype=jnp.int32)[None, :]).astype(
        jnp.int32
    )
    before = jnp.cumsum(onehot, axis=0) - onehot
    return jnp.sum(before * onehot, axis=1).reshape(id_table.shape)


def body(tokens, norm_gain, expert_ids, route_weights, gate_proj, up_proj, down_proj):
    dp_count = lax.axis_size("dp")
    expert_count = lax.axis_size("expert")
    local_experts = gate_proj.shape[0]
    model_width = tokens.shape[2]
    group_ids = expert_ids[0]
    group_weights = route_weights[0]
    group_size = group_ids.shape[0]
    own_rows = group_size // dp_count
    top_k = group_ids.shape[1]
    experts = local_experts * expert_count
    capacity = dp_count * (group_size * top_k // (experts * dp_count) + 1)
    tok_float = tokens[0].astype(jnp.float32)
    inv_rms = lax.rsqrt(jnp.mean(tok_float * tok_float, axis=-1, keepdims=True) + 1e-06)
    group_rows = (tok_float * inv_rms * norm_gain).astype(jnp.bfloat16)
    slot_rank = rank_slots(group_ids, experts)
    slot_index = group_ids * capacity + slot_rank
    token_order = jnp.broadcast_to(
        jnp.arange(group_size, dtype=jnp.int32)[:, None], (group_size, top_k)
    )
    sources = (
        jnp.full((experts * capacity,), group_size, jnp.int32)
        .at[slot_index.reshape(-1)]
        .set(token_order.reshape(-1))
    )
    padded = jnp.concatenate([group_rows, jnp.zeros((1, model_width), jnp.bfloat16)], axis=0)
    outgoing = jnp.take(padded, sources, axis=0).reshape(
        expert_count, local_experts, capacity, model_width
    )
    incoming = lax.all_to_all(outgoing, "expert", split_axis=0, concat_axis=0, tiled=True)
    gate_act = jnp.einsum("sjmd,jfd->sjmf", incoming, gate_proj, preferred_element_type=jnp.float32)
    up_act = jnp.einsum("sjmd,jfd->sjmf", incoming, up_proj, preferred_element_type=jnp.float32)
    hidden = (jax.nn.silu(gate_act) * up_act).astype(jnp.bfloat16)
    partial_rows = jnp.einsum(
        "sjmf,jfd->sjmd", hidden, down_proj, preferred_element_type=jnp.float32
    ).astype(jnp.bfloat16)
    returned = lax.all_to_all(partial_rows, "expert", split_axis=0, concat_axis=0, tiled=True)
    lookup = jnp.concatenate(
        [
            returned.reshape(experts * capacity, model_width),
            jnp.zeros((1, model_width), jnp.bfloat16),
        ],
        axis=0,
    )
    picked = (
        jnp.take(lookup, slot_index.reshape(-1), axis=0)
        .reshape(own_rows * lax.axis_size("dp"), top_k, model_width)
        .astype(jnp.float32)
    )
    mixed = lax.psum_scatter(
        jnp.sum(picked * group_weights[:, :, None], axis=1).astype(jnp.bfloat16),
        "dp",
        scatter_dimension=0,
        tiled=True,
    )
    return mixed[None]


def solution(mesh):
    placed = (
        P("expert", None, None),
        P(),
        P("expert", None, None),
        P("expert", None, None),
        P("expert", "dp", None),
        P("expert", "dp", None),
        P("expert", "dp", None),
    )
    small = mesh.shape["expert"] == 8 and mesh.shape["dp"] == 4
    return jax.shard_map(
        fused_body if small else body, mesh=mesh, in_specs=placed, out_specs=P("expert", "dp", None), check_vma=False
    )
```

```python
import functools

import jax
import jax.numpy as jnp
from jax import lax
from jax.experimental import pallas as pl
from jax.experimental.pallas import tpu as pltpu
from jax.sharding import PartitionSpec as P

MESH = pl.DeviceIdType.MESH
BATCHES = 2
IN_CHUNKS = 2
OUT_CHUNKS = 4
IN_STEPS = BATCHES * IN_CHUNKS
OUT_STEPS = BATCHES * OUT_CHUNKS
OWN, ALONG_X, ALONG_Y, DIAGONAL, SIBLING = 0, 1, 2, 3, 4


def fused(
    dp_count,
    local_experts,
    tok_ref,
    gain_ref,
    dense_ref,
    gate_hbm,
    up_hbm,
    down_hbm,
    out_ref,
    w_in,
    w_out,
    rows,
    flipped,
    dense,
    acc,
    hidden,
    to_sib,
    kept,
    from_sib,
    to_x,
    to_y,
    from_x,
    from_y,
    to_x2,
    to_y2,
    from_x2,
    from_y2,
    summed,
    to_z,
    from_z,
    result,
    w_sem,
    d_send,
    d_recv,
    a_send,
    a_recv,
    r_send,
    r_recv,
):
    me = lax.axis_index("expert")
    plane = lax.axis_index("dp")
    sib = me + 1 - 2 * lax.rem(me, 2)
    nx = me + 2 - 4 * lax.rem(me // 2, 2)
    ny = me + 4 - 8 * (me // 4)
    token_count, width = tok_ref.shape
    in_span = width // IN_CHUNKS
    out_span = width // OUT_CHUNKS
    batch = token_count // BATCHES
    half = batch // 2
    own = token_count // dp_count
    piece = own // BATCHES
    hid = w_out.shape[0]
    all_rows = 8 * batch
    core_rows = 4 * batch

    loads = [
        pltpu.make_async_copy(gate_hbm, w_in.at[pl.ds(0, hid)], w_sem.at[0]),
        pltpu.make_async_copy(up_hbm, w_in.at[pl.ds(hid, hid)], w_sem.at[1]),
        pltpu.make_async_copy(down_hbm, w_out, w_sem.at[2]),
    ]
    for load in loads:
        load.start()

    barrier = pltpu.get_barrier_semaphore()
    for peer in (sib, nx, ny):
        pl.semaphore_signal(barrier, inc=1, device_id={"expert": peer}, device_id_type=MESH)
    for step in range(1, dp_count):
        pl.semaphore_signal(
            barrier,
            inc=1,
            device_id={"dp": lax.rem(plane + step, dp_count)},
            device_id_type=MESH,
        )

    tok = tok_ref[...].astype(jnp.float32)
    inv_rms = lax.rsqrt(jnp.mean(tok * tok, axis=-1, keepdims=True) + 1e-06)
    for c in range(IN_CHUNKS):
        cols = slice(c * in_span, (c + 1) * in_span)
        part = tok_ref[:, cols].astype(jnp.float32) * inv_rms * gain_ref[:, cols]
        for b in range(BATCHES):
            picked = [
                part[z * own + b * piece : z * own + (b + 1) * piece] for z in range(dp_count)
            ]
            rows[b * IN_CHUNKS + c, OWN] = jnp.concatenate(picked, axis=0).astype(jnp.bfloat16)
    dense[OWN] = jnp.zeros(dense.shape[1:], dense.dtype)
    dense[OWN, :, :token_count] = dense_ref[...]

    pl.semaphore_wait(barrier, 3 + dp_count - 1)

    def push(src, dst, send, recv, **where):
        return pltpu.make_async_remote_copy(
            src_ref=src,
            dst_ref=dst,
            send_sem=send,
            recv_sem=recv,
            device_id=where,
            device_id_type=MESH,
        )

    def dense_push(k, src, dst, peer):
        return push(dense.at[src], dense.at[dst], d_send.at[k], d_recv.at[k], expert=peer)

    dense_copies = [
        dense_push(0, OWN, ALONG_X, nx),
        dense_push(1, OWN, ALONG_Y, ny),
        dense_push(2, OWN, SIBLING, sib),
        dense_push(3, ALONG_X, DIAGONAL, ny),
        dense_push(4, ALONG_X, SIBLING + ALONG_X, sib),
        dense_push(5, ALONG_Y, SIBLING + ALONG_Y, sib),
        dense_push(6, DIAGONAL, SIBLING + DIAGONAL, sib),
    ]

    spread = dp_count * 128
    straight = in_span - spread
    block_at = pl.multiple_of(straight + plane * 128, 128)
    main_cols = pl.ds(0, straight)
    plane_cols = pl.ds(block_at, 128)
    spread_cols = pl.ds(straight, spread)

    def gather_copies(s):
        def go(k, src, dst, cols, part=None, **where):
            lines = pl.ds(0, batch) if part is None else pl.ds(part * half, half)
            return push(
                rows.at[s, src, lines, cols],
                rows.at[s, dst, lines, cols],
                a_send.at[s, k],
                a_recv.at[s, k],
                **where,
            )

        every = pl.ds(0, in_span)
        remote = pl.ds(ALONG_X, 3)
        copies = [
            go(0, OWN, ALONG_X, main_cols, expert=nx),
            go(1, OWN, ALONG_Y, main_cols, expert=ny),
            go(2, OWN, SIBLING, every, expert=sib),
            go(3, ALONG_X, DIAGONAL, main_cols, 0, expert=ny),
            go(4, ALONG_Y, DIAGONAL, main_cols, 1, expert=nx),
            go(5, ALONG_X, SIBLING + ALONG_X, main_cols, expert=sib),
            go(6, ALONG_Y, SIBLING + ALONG_Y, main_cols, expert=sib),
            go(7, DIAGONAL, SIBLING + DIAGONAL, main_cols, expert=sib),
            go(8, OWN, ALONG_X, plane_cols, expert=nx),
            go(9, OWN, ALONG_Y, plane_cols, expert=ny),
            go(10, ALONG_X, DIAGONAL, plane_cols, 0, expert=ny),
            go(11, ALONG_Y, DIAGONAL, plane_cols, 1, expert=nx),
            go(12, remote, pl.ds(SIBLING + ALONG_X, 3), spread_cols, expert=sib),
        ]
        for step in range(1, dp_count):
            peer = lax.rem(plane + step, dp_count)
            copies.append(go(12 + step, remote, remote, plane_cols, dp=peer))
        return copies

    gather = [gather_copies(s) for s in range(IN_STEPS)]
    for k in range(3):
        dense_copies[k].start()

    def share(s):
        for k in (8, 9, 0, 1, 2):
            gather[s][k].start()

    share(0)
    share(1)

    def forward(s):
        copies = gather[s]
        copies[8].wait_recv()
        copies[10].start()
        copies[9].wait_recv()
        copies[11].start()
        copies[0].wait_recv()
        copies[3].start()
        copies[5].start()
        copies[1].wait_recv()
        copies[4].start()
        copies[6].start()
        copies[10].wait_recv()
        copies[11].wait_recv()
        for step in range(1, dp_count):
            copies[12 + step].start()

    def forward_diagonal(s):
        copies = gather[s]
        copies[3].wait_recv()
        copies[4].wait_recv()
        copies[7].start()
        for step in range(1, dp_count):
            copies[12 + step].wait_recv()
        copies[12].start()

    def multiply_in(s):
        c = s % IN_CHUNKS
        for k in (2, 5, 6, 7, 12):
            gather[s][k].wait_recv()
        flipped[...] = rows[s].reshape(all_rows, in_span).T

        @pl.loop(0, 2)
        def _(t):
            w = w_in[
                pl.ds(pl.multiple_of(t * hid, hid), hid), c * in_span : (c + 1) * in_span
            ]
            y = jnp.dot(w, flipped[...], preferred_element_type=jnp.float32)
            if c == 0:
                acc[t] = y
            else:
                acc[t] += y

    expert_rows = lax.broadcasted_iota(jnp.int32, dense.shape[1:], 0)
    per_expert = hid // local_experts

    def activate(b):
        for j in range(local_experts):
            scale = jnp.concatenate(
                [
                    jnp.sum(
                        jnp.where(expert_rows == me * local_experts + j, dense[p], 0.0),
                        axis=0,
                        keepdims=True,
                    )[:, b * batch : (b + 1) * batch]
                    for p in range(8)
                ],
                axis=1,
            )
            for k in range(j * per_expert, (j + 1) * per_expert, 128):
                g = acc[0, k : k + 128]
                h = g / (1.0 + jnp.exp(-g)) * acc[1, k : k + 128] * scale
                hidden[:, k : k + 128] = h.astype(jnp.bfloat16).T

    def reduce_copies(n):
        def go(k, src, dst, **where):
            return push(src, dst, r_send.at[n, k], r_recv.at[n, k], **where)

        copies = [
            go(0, to_sib.at[n], from_sib.at[n], expert=sib),
            go(1, to_x.at[n], from_x.at[n], expert=nx),
            go(2, to_y.at[n], from_y.at[n], expert=ny),
            go(3, to_y2.at[n], from_y2.at[n], expert=ny),
            go(4, to_x2.at[n], from_x2.at[n], expert=nx),
        ]
        for step in range(1, dp_count):
            peer = lax.rem(plane + step, dp_count)
            copies.append(go(4 + step, to_z.at[n, peer], from_z.at[n, step - 1], dp=peer))
        return copies

    reduce = [reduce_copies(n) for n in range(OUT_STEPS)]

    def multiply_out(n):
        step = 512

        @pl.loop(0, out_span // step)
        def _(t):
            w = w_out[:, pl.ds(pl.multiple_of(n % OUT_CHUNKS * out_span + t * step, step), step)]
            y = jnp.dot(hidden[...], w, preferred_element_type=jnp.float32)
            cols = pl.ds(pl.multiple_of(t * step, step), step)
            to_sib[n, :, cols] = y[core_rows:].astype(jnp.bfloat16)
            kept[n, :, cols] = y[:core_rows]

        reduce[n][0].start()

    def block(place, part):
        return slice(place * batch + part * half, place * batch + (part + 1) * half)

    def pair_sum(n):
        reduce[n][0].wait_recv()

        def total(place, part):
            at = block(place, part)
            return kept[n, at] + from_sib[n, at].astype(jnp.float32)

        to_x[n, :half] = total(ALONG_X, 0).astype(jnp.bfloat16)
        to_x[n, half:] = total(DIAGONAL, 0).astype(jnp.bfloat16)
        reduce[n][1].start()
        to_y[n, :half] = total(ALONG_Y, 1).astype(jnp.bfloat16)
        to_y[n, half:] = total(DIAGONAL, 1).astype(jnp.bfloat16)
        reduce[n][2].start()
        for place, part in ((OWN, 0), (OWN, 1), (ALONG_Y, 0), (ALONG_X, 1)):
            kept[n, block(place, part)] = total(place, part)

    def second_hop(n):
        reduce[n][1].wait_recv()
        to_y2[n] = (
            kept[n, block(ALONG_Y, 0)] + from_x[n, half:].astype(jnp.float32)
        ).astype(jnp.bfloat16)
        reduce[n][3].start()
        reduce[n][2].wait_recv()
        to_x2[n] = (
            kept[n, block(ALONG_X, 1)] + from_y[n, half:].astype(jnp.float32)
        ).astype(jnp.bfloat16)
        reduce[n][4].start()

    def across_planes(n):
        reduce[n][3].wait_recv()
        reduce[n][4].wait_recv()
        first = (
            kept[n, block(OWN, 0)]
            + from_x[n, :half].astype(jnp.float32)
            + from_y2[n].astype(jnp.float32)
        )
        second = (
            kept[n, block(OWN, 1)]
            + from_y[n, :half].astype(jnp.float32)
            + from_x2[n].astype(jnp.float32)
        )
        per_half = half // piece
        for i in range(dp_count):
            source = first if i < per_half else second
            at = i % per_half * piece
            rows_i = source[at : at + piece]
            folded = jnp.concatenate(
                [rows_i[:, f * fold : (f + 1) * fold] for f in range(BATCHES)], axis=0
            )
            summed[n, i] = folded
            to_z[n, i] = folded.astype(jnp.bfloat16)
        for step in range(1, dp_count):
            reduce[n][4 + step].start()

    fold = out_span // BATCHES

    def finish(n):
        total = summed[n, plane]
        for step in range(1, dp_count):
            reduce[n][4 + step].wait_recv()
            total = total + from_z[n, step - 1].astype(jnp.float32)
        b, c = n // OUT_CHUNKS, n % OUT_CHUNKS
        for f in range(BATCHES):
            at = c * out_span + f * fold
            result[b * piece : (b + 1) * piece, at : at + fold] = total[
                f * piece : (f + 1) * piece
            ]

    forward(0)
    share(2)
    dense_copies[0].wait_recv()
    dense_copies[3].start()
    dense_copies[4].start()
    dense_copies[1].wait_recv()
    dense_copies[5].start()
    forward(1)
    share(3)
    forward_diagonal(0)
    dense_copies[3].wait_recv()
    dense_copies[6].start()
    loads[0].wait()
    loads[1].wait()
    multiply_in(0)
    forward_diagonal(1)
    forward(2)
    multiply_in(1)
    for k in (2, 4, 5, 6):
        dense_copies[k].wait_recv()
    activate(0)
    loads[2].wait()
    multiply_out(0)
    multiply_out(1)
    forward(3)
    multiply_out(2)
    pair_sum(0)
    multiply_out(3)
    pair_sum(1)
    forward_diagonal(2)
    multiply_in(2)
    pair_sum(2)
    pair_sum(3)
    forward_diagonal(3)
    multiply_in(3)
    second_hop(0)
    second_hop(1)
    activate(1)
    multiply_out(4)
    second_hop(2)
    multiply_out(5)
    pair_sum(4)
    second_hop(3)
    multiply_out(6)
    pair_sum(5)
    across_planes(0)
    multiply_out(7)
    pair_sum(6)
    across_planes(1)
    pair_sum(7)
    across_planes(2)
    across_planes(3)
    second_hop(4)
    finish(0)
    second_hop(5)
    finish(1)
    across_planes(4)
    second_hop(6)
    finish(2)
    across_planes(5)
    second_hop(7)
    finish(3)
    across_planes(6)
    finish(4)
    across_planes(7)
    finish(5)
    finish(6)
    finish(7)
    out_ref[...] = result[...].astype(jnp.bfloat16)

    for copy in dense_copies:
        copy.wait_send()
    for copies in gather + reduce:
        for copy in copies:
            copy.wait_send()


def fused_body(tokens, norm_gain, expert_ids, route_weights, gate_proj, up_proj, down_proj):
    dp_count = lax.axis_size("dp")
    local_experts, block_hid, width = gate_proj.shape
    experts = local_experts * lax.axis_size("expert")
    token_count = tokens.shape[1]
    hid = local_experts * block_hid
    in_span = width // IN_CHUNKS
    out_span = width // OUT_CHUNKS
    batch = token_count // BATCHES
    half = batch // 2
    own = token_count // dp_count
    core_rows = 4 * batch

    def regroup(table):
        pieces = table.reshape(dp_count, BATCHES, own // BATCHES, table.shape[1])
        return pieces.swapaxes(0, 1).reshape(table.shape).T[None]

    named = regroup(expert_ids[0]) == jnp.arange(experts, dtype=jnp.int32)[:, None, None]
    dense = jnp.sum(jnp.where(named, regroup(route_weights[0]), 0.0), axis=1)

    bf16, f32 = jnp.bfloat16, jnp.float32
    vmem = pl.BlockSpec(memory_space=pltpu.VMEM)
    anywhere = pl.BlockSpec(memory_space=pl.ANY)
    dma = pltpu.SemaphoreType.DMA
    mixed = pl.pallas_call(
        functools.partial(fused, dp_count, local_experts),
        out_shape=jax.ShapeDtypeStruct((own, width), bf16),
        in_specs=[vmem] * 3 + [anywhere] * 3,
        out_specs=vmem,
        scratch_shapes=[
            pltpu.VMEM((2 * hid, width), bf16),
            pltpu.VMEM((hid, width), bf16),
            pltpu.VMEM((IN_STEPS, 8, batch, in_span), bf16),
            pltpu.VMEM((in_span, 8 * batch), bf16),
            pltpu.VMEM((8, experts, 128), f32),
            pltpu.VMEM((2, hid, 8 * batch), f32),
            pltpu.VMEM((8 * batch, hid), bf16),
            pltpu.VMEM((OUT_STEPS, core_rows, out_span), bf16),
            pltpu.VMEM((OUT_STEPS, core_rows, out_span), f32),
            pltpu.VMEM((OUT_STEPS, core_rows, out_span), bf16),
            pltpu.VMEM((OUT_STEPS, 2 * half, out_span), bf16),
            pltpu.VMEM((OUT_STEPS, 2 * half, out_span), bf16),
            pltpu.VMEM((OUT_STEPS, 2 * half, out_span), bf16),
            pltpu.VMEM((OUT_STEPS, 2 * half, out_span), bf16),
            pltpu.VMEM((OUT_STEPS, half, out_span), bf16),
            pltpu.VMEM((OUT_STEPS, half, out_span), bf16),
            pltpu.VMEM((OUT_STEPS, half, out_span), bf16),
            pltpu.VMEM((OUT_STEPS, half, out_span), bf16),
            pltpu.VMEM((OUT_STEPS, dp_count, own, out_span // BATCHES), f32),
            pltpu.VMEM((OUT_STEPS, dp_count, own, out_span // BATCHES), bf16),
            pltpu.VMEM((OUT_STEPS, dp_count - 1, own, out_span // BATCHES), bf16),
            pltpu.VMEM((own, width), f32),
            dma((3,)),
            dma((7,)),
            dma((7,)),
            dma((IN_STEPS, 12 + dp_count)),
            dma((IN_STEPS, 12 + dp_count)),
            dma((OUT_STEPS, 4 + dp_count)),
            dma((OUT_STEPS, 4 + dp_count)),
        ],
        compiler_params=pltpu.CompilerParams(
            collective_id=0, has_side_effects=True, vmem_limit_bytes=56 * 1024 * 1024
        ),
        cost_estimate=pl.CostEstimate(
            flops=2 * 3 * 8 * token_count * hid * width,
            bytes_accessed=3 * hid * width * 2,
            transcendentals=8 * token_count * hid,
        ),
    )(
        tokens[0],
        norm_gain[None],
        dense,
        gate_proj.reshape(hid, width),
        up_proj.reshape(hid, width),
        down_proj.reshape(hid, width),
    )
    return mixed[None]


def rank_slots(id_table, expert_total):
    flat_ids = id_table.reshape(-1)
    onehot = (flat_ids[:, None] == jnp.arange(expert_total, dtype=jnp.int32)[None, :]).astype(
        jnp.int32
    )
    before = jnp.cumsum(onehot, axis=0) - onehot
    return jnp.sum(before * onehot, axis=1).reshape(id_table.shape)


def body(tokens, norm_gain, expert_ids, route_weights, gate_proj, up_proj, down_proj):
    dp_count = lax.axis_size("dp")
    expert_count = lax.axis_size("expert")
    local_experts = gate_proj.shape[0]
    model_width = tokens.shape[2]
    group_ids = expert_ids[0]
    group_weights = route_weights[0]
    group_size = group_ids.shape[0]
    own_rows = group_size // dp_count
    top_k = group_ids.shape[1]
    experts = local_experts * expert_count
    capacity = dp_count * (group_size * top_k // (experts * dp_count) + 1)
    tok_float = tokens[0].astype(jnp.float32)
    inv_rms = lax.rsqrt(jnp.mean(tok_float * tok_float, axis=-1, keepdims=True) + 1e-06)
    group_rows = (tok_float * inv_rms * norm_gain).astype(jnp.bfloat16)
    slot_rank = rank_slots(group_ids, experts)
    slot_index = group_ids * capacity + slot_rank
    token_order = jnp.broadcast_to(
        jnp.arange(group_size, dtype=jnp.int32)[:, None], (group_size, top_k)
    )
    sources = (
        jnp.full((experts * capacity,), group_size, jnp.int32)
        .at[slot_index.reshape(-1)]
        .set(token_order.reshape(-1))
    )
    padded = jnp.concatenate([group_rows, jnp.zeros((1, model_width), jnp.bfloat16)], axis=0)
    outgoing = jnp.take(padded, sources, axis=0).reshape(
        expert_count, local_experts, capacity, model_width
    )
    incoming = lax.all_to_all(outgoing, "expert", split_axis=0, concat_axis=0, tiled=True)
    gate_act = jnp.einsum("sjmd,jfd->sjmf", incoming, gate_proj, preferred_element_type=jnp.float32)
    up_act = jnp.einsum("sjmd,jfd->sjmf", incoming, up_proj, preferred_element_type=jnp.float32)
    hidden = (jax.nn.silu(gate_act) * up_act).astype(jnp.bfloat16)
    partial_rows = jnp.einsum(
        "sjmf,jfd->sjmd", hidden, down_proj, preferred_element_type=jnp.float32
    ).astype(jnp.bfloat16)
    returned = lax.all_to_all(partial_rows, "expert", split_axis=0, concat_axis=0, tiled=True)
    lookup = jnp.concatenate(
        [
            returned.reshape(experts * capacity, model_width),
            jnp.zeros((1, model_width), jnp.bfloat16),
        ],
        axis=0,
    )
    picked = (
        jnp.take(lookup, slot_index.reshape(-1), axis=0)
        .reshape(own_rows * lax.axis_size("dp"), top_k, model_width)
        .astype(jnp.float32)
    )
    mixed = lax.psum_scatter(
        jnp.sum(picked * group_weights[:, :, None], axis=1).astype(jnp.bfloat16),
        "dp",
        scatter_dimension=0,
        tiled=True,
    )
    return mixed[None]


def solution(mesh):
    placed = (
        P("expert", None, None),
        P(),
        P("expert", None, None),
        P("expert", None, None),
        P("expert", "dp", None),
        P("expert", "dp", None),
        P("expert", "dp", None),
    )
    small = mesh.shape["expert"] == 8 and mesh.shape["dp"] == 4
    return jax.shard_map(
        fused_body if small else body, mesh=mesh, in_specs=placed, out_specs=P("expert", "dp", None), check_vma=False
    )
```

```python
import functools

import jax
import jax.numpy as jnp
from jax import lax
from jax.experimental import pallas as pl
from jax.experimental.pallas import tpu as pltpu
from jax.sharding import PartitionSpec as P

MESH = pl.DeviceIdType.MESH
BATCHES = 2
IN_CHUNKS = 2
OUT_CHUNKS = 4
IN_STEPS = BATCHES * IN_CHUNKS
OUT_STEPS = BATCHES * OUT_CHUNKS
OWN, ALONG_X, ALONG_Y, DIAGONAL, SIBLING = 0, 1, 2, 3, 4


def fused(
    dp_count,
    local_experts,
    tok_ref,
    gain_ref,
    ids_ref,
    route_ref,
    gate_hbm,
    up_hbm,
    down_hbm,
    out_ref,
    w_in,
    w_out,
    rows,
    flipped,
    dense,
    acc,
    hidden,
    to_sib,
    kept,
    from_sib,
    to_x,
    to_y,
    from_x,
    from_y,
    to_x2,
    to_y2,
    from_x2,
    from_y2,
    summed,
    to_z,
    from_z,
    w_sem,
    d_send,
    d_recv,
    a_send,
    a_recv,
    r_send,
    r_recv,
):
    me = lax.axis_index("expert")
    plane = lax.axis_index("dp")
    sib = me + 1 - 2 * lax.rem(me, 2)
    nx = me + 2 - 4 * lax.rem(me // 2, 2)
    ny = me + 4 - 8 * (me // 4)
    token_count, width = tok_ref.shape
    in_span = width // IN_CHUNKS
    out_span = width // OUT_CHUNKS
    batch = token_count // BATCHES
    half = batch // 2
    own = token_count // dp_count
    piece = own // BATCHES
    hid = w_out.shape[0]
    all_rows = 8 * batch
    core_rows = 4 * batch

    loads = [
        pltpu.make_async_copy(gate_hbm, w_in.at[pl.ds(0, hid)], w_sem.at[0]),
        pltpu.make_async_copy(up_hbm, w_in.at[pl.ds(hid, hid)], w_sem.at[1]),
        pltpu.make_async_copy(down_hbm, w_out, w_sem.at[2]),
    ]
    for load in loads:
        load.start()

    barrier = pltpu.get_barrier_semaphore()
    for peer in (sib, nx, ny):
        pl.semaphore_signal(barrier, inc=1, device_id={"expert": peer}, device_id_type=MESH)
    for step in range(1, dp_count):
        pl.semaphore_signal(
            barrier,
            inc=1,
            device_id={"dp": lax.rem(plane + step, dp_count)},
            device_id_type=MESH,
        )

    for c in range(IN_CHUNKS):
        cols = slice(c * in_span, (c + 1) * in_span)
        part = tok_ref[:, cols].astype(jnp.float32) * gain_ref[:, cols]
        for b in range(BATCHES):
            picked = [
                part[z * own + b * piece : z * own + (b + 1) * piece] for z in range(dp_count)
            ]
            rows[b * IN_CHUNKS + c, OWN] = jnp.concatenate(picked, axis=0).astype(jnp.bfloat16)
    pl.semaphore_wait(barrier, 3 + dp_count - 1)

    def push(src, dst, send, recv, **where):
        return pltpu.make_async_remote_copy(
            src_ref=src,
            dst_ref=dst,
            send_sem=send,
            recv_sem=recv,
            device_id=where,
            device_id_type=MESH,
        )

    def dense_push(k, src, dst, peer):
        return push(dense.at[src], dense.at[dst], d_send.at[k], d_recv.at[k], expert=peer)

    dense_copies = [
        dense_push(0, OWN, ALONG_X, nx),
        dense_push(1, OWN, ALONG_Y, ny),
        dense_push(2, OWN, SIBLING, sib),
        dense_push(3, ALONG_X, DIAGONAL, ny),
        dense_push(4, ALONG_X, SIBLING + ALONG_X, sib),
        dense_push(5, ALONG_Y, SIBLING + ALONG_Y, sib),
        dense_push(6, DIAGONAL, SIBLING + DIAGONAL, sib),
    ]

    def gather_copies(c):
        def go(k, src, dst, peer, part=None):
            a, b = rows.at[c, src], rows.at[c, dst]
            if part is not None:
                a = rows.at[c, src, pl.ds(part * half, half)]
                b = rows.at[c, dst, pl.ds(part * half, half)]
            return push(a, b, a_send.at[c, k], a_recv.at[c, k], expert=peer)

        return [
            go(0, OWN, ALONG_X, nx),
            go(1, OWN, ALONG_Y, ny),
            go(2, OWN, SIBLING, sib),
            go(3, ALONG_X, DIAGONAL, ny, 0),
            go(4, ALONG_Y, DIAGONAL, nx, 1),
            go(5, ALONG_X, SIBLING + ALONG_X, sib),
            go(6, ALONG_Y, SIBLING + ALONG_Y, sib),
            go(7, DIAGONAL, SIBLING + DIAGONAL, sib),
        ]

    gather = [gather_copies(s) for s in range(IN_STEPS)]

    def share(s):
        for k in range(3):
            gather[s][k].start()

    share(0)
    share(1)

    tok = tok_ref[...].astype(jnp.float32)
    inv_rms = lax.rsqrt(jnp.mean(tok * tok, axis=-1, keepdims=True) + 1e-06)
    token = lax.broadcasted_iota(jnp.int32, (token_count, 128), 0)
    lane = lax.broadcasted_iota(jnp.int32, (token_count, 128), 1)
    within = lax.rem(token, own)
    ordered = lane == (within // piece) * batch + (token // own) * piece + lax.rem(within, piece)
    experts = dense.shape[1] - 8

    def regroup(by_choice):
        starts = [z * own + b * piece for b in range(BATCHES) for z in range(dp_count)]
        return jnp.concatenate([by_choice[:, at : at + piece] for at in starts], axis=1)

    ids, route = regroup(ids_ref[...]), regroup(route_ref[...])
    table = [
        jnp.sum(jnp.where(ids == e, route, 0.0), axis=0, keepdims=True) for e in range(experts)
    ]
    dense[OWN] = jnp.zeros(dense.shape[1:], dense.dtype)
    dense[OWN, :experts, :token_count] = jnp.concatenate(table, axis=0)
    inv_row = jnp.sum(jnp.where(ordered, inv_rms, 0.0), axis=0, keepdims=True)
    dense[OWN, experts:] = jnp.broadcast_to(inv_row, (8, 128))
    for k in range(3):
        dense_copies[k].start()

    def forward(c):
        gather[c][0].wait_recv()
        gather[c][3].start()
        gather[c][5].start()
        gather[c][1].wait_recv()
        gather[c][4].start()
        gather[c][6].start()

    def forward_diagonal(c):
        gather[c][3].wait_recv()
        gather[c][4].wait_recv()
        gather[c][7].start()

    def multiply_in(s):
        c = s % IN_CHUNKS
        for k in (2, 5, 6, 7):
            gather[s][k].wait_recv()
        flipped[...] = rows[s].reshape(all_rows, in_span).T

        @pl.loop(0, 2)
        def _(t):
            w = w_in[
                pl.ds(pl.multiple_of(t * hid, hid), hid), c * in_span : (c + 1) * in_span
            ]
            y = jnp.dot(w, flipped[...], preferred_element_type=jnp.float32)
            if c == 0:
                acc[t] = y
            else:
                acc[t] += y

    expert_rows = lax.broadcasted_iota(jnp.int32, dense.shape[1:], 0)
    per_expert = hid // local_experts

    def batch_row(b, row):
        picked = [
            jnp.sum(jnp.where(expert_rows == row, dense[p], 0.0), axis=0, keepdims=True)
            for p in range(8)
        ]
        return jnp.concatenate([r[:, b * batch : (b + 1) * batch] for r in picked], axis=1)

    def activate(b):
        inv = batch_row(b, experts)
        for j in range(local_experts):
            scale = inv * batch_row(b, me * local_experts + j)
            for k in range(j * per_expert, (j + 1) * per_expert, 128):
                g = acc[0, k : k + 128] * inv
                h = g / (1.0 + jnp.exp(-g)) * (acc[1, k : k + 128] * scale)
                hidden[:, k : k + 128] = h.astype(jnp.bfloat16).T

    def reduce_copies(n):
        def go(k, src, dst, **where):
            return push(src, dst, r_send.at[n, k], r_recv.at[n, k], **where)

        copies = [
            go(0, to_sib.at[n], from_sib.at[n], expert=sib),
            go(1, to_x.at[n], from_x.at[n], expert=nx),
            go(2, to_y.at[n], from_y.at[n], expert=ny),
            go(3, to_y2.at[n], from_y2.at[n], expert=ny),
            go(4, to_x2.at[n], from_x2.at[n], expert=nx),
        ]
        for step in range(1, dp_count):
            peer = lax.rem(plane + step, dp_count)
            copies.append(go(4 + step, to_z.at[n, peer], from_z.at[n, step - 1], dp=peer))
        return copies

    reduce = [reduce_copies(n) for n in range(OUT_STEPS)]

    def multiply_out(n):
        step = 512

        @pl.loop(0, out_span // step)
        def _(t):
            w = w_out[:, pl.ds(pl.multiple_of(n % OUT_CHUNKS * out_span + t * step, step), step)]
            y = jnp.dot(hidden[...], w, preferred_element_type=jnp.float32)
            cols = pl.ds(pl.multiple_of(t * step, step), step)
            to_sib[n, :, cols] = y[core_rows:].astype(jnp.bfloat16)
            kept[n, :, cols] = y[:core_rows]

        reduce[n][0].start()

    def block(place, part):
        return slice(place * batch + part * half, place * batch + (part + 1) * half)

    def pair_sum(n):
        reduce[n][0].wait_recv()

        def total(place, part):
            at = block(place, part)
            return kept[n, at] + from_sib[n, at].astype(jnp.float32)

        to_x[n, :half] = total(ALONG_X, 0).astype(jnp.bfloat16)
        to_x[n, half:] = total(DIAGONAL, 0).astype(jnp.bfloat16)
        reduce[n][1].start()
        to_y[n, :half] = total(ALONG_Y, 1).astype(jnp.bfloat16)
        to_y[n, half:] = total(DIAGONAL, 1).astype(jnp.bfloat16)
        reduce[n][2].start()
        for place, part in ((OWN, 0), (OWN, 1), (ALONG_Y, 0), (ALONG_X, 1)):
            kept[n, block(place, part)] = total(place, part)

    def second_hop(n):
        reduce[n][1].wait_recv()
        to_y2[n] = (
            kept[n, block(ALONG_Y, 0)] + from_x[n, half:].astype(jnp.float32)
        ).astype(jnp.bfloat16)
        reduce[n][3].start()
        reduce[n][2].wait_recv()
        to_x2[n] = (
            kept[n, block(ALONG_X, 1)] + from_y[n, half:].astype(jnp.float32)
        ).astype(jnp.bfloat16)
        reduce[n][4].start()

    def across_planes(n):
        reduce[n][3].wait_recv()
        reduce[n][4].wait_recv()
        first = (
            kept[n, block(OWN, 0)]
            + from_x[n, :half].astype(jnp.float32)
            + from_y2[n].astype(jnp.float32)
        )
        second = (
            kept[n, block(OWN, 1)]
            + from_y[n, :half].astype(jnp.float32)
            + from_x2[n].astype(jnp.float32)
        )
        per_half = half // piece
        for i in range(dp_count):
            source = first if i < per_half else second
            at = i % per_half * piece
            rows_i = source[at : at + piece]
            folded = jnp.concatenate(
                [rows_i[:, f * fold : (f + 1) * fold] for f in range(BATCHES)], axis=0
            )
            summed[n, i] = folded
            to_z[n, i] = folded.astype(jnp.bfloat16)
        for step in range(1, dp_count):
            reduce[n][4 + step].start()

    fold = out_span // BATCHES

    def finish(n):
        total = summed[n, plane]
        for step in range(1, dp_count):
            reduce[n][4 + step].wait_recv()
            total = total + from_z[n, step - 1].astype(jnp.float32)
        b, c = n // OUT_CHUNKS, n % OUT_CHUNKS
        for f in range(BATCHES):
            at = c * out_span + f * fold
            out_ref[b * piece : (b + 1) * piece, at : at + fold] = total[
                f * piece : (f + 1) * piece
            ]

    forward(0)
    share(2)
    dense_copies[0].wait_recv()
    dense_copies[3].start()
    dense_copies[4].start()
    dense_copies[1].wait_recv()
    dense_copies[5].start()
    forward(1)
    share(3)
    forward_diagonal(0)
    dense_copies[3].wait_recv()
    dense_copies[6].start()
    loads[0].wait()
    loads[1].wait()
    multiply_in(0)
    forward_diagonal(1)
    forward(2)
    multiply_in(1)
    for k in (2, 4, 5, 6):
        dense_copies[k].wait_recv()
    activate(0)
    loads[2].wait()
    multiply_out(0)
    multiply_out(1)
    forward(3)
    multiply_out(2)
    pair_sum(0)
    multiply_out(3)
    pair_sum(1)
    forward_diagonal(2)
    multiply_in(2)
    pair_sum(2)
    pair_sum(3)
    forward_diagonal(3)
    multiply_in(3)
    second_hop(0)
    second_hop(1)
    activate(1)
    multiply_out(4)
    second_hop(2)
    multiply_out(5)
    pair_sum(4)
    second_hop(3)
    multiply_out(6)
    pair_sum(5)
    across_planes(0)
    multiply_out(7)
    pair_sum(6)
    across_planes(1)
    pair_sum(7)
    across_planes(2)
    across_planes(3)
    second_hop(4)
    finish(0)
    second_hop(5)
    finish(1)
    across_planes(4)
    second_hop(6)
    finish(2)
    across_planes(5)
    second_hop(7)
    finish(3)
    across_planes(6)
    finish(4)
    across_planes(7)
    finish(5)
    finish(6)
    finish(7)

    for copy in dense_copies:
        copy.wait_send()
    for copies in gather + reduce:
        for copy in copies:
            copy.wait_send()


def fused_body(tokens, norm_gain, expert_ids, route_weights, gate_proj, up_proj, down_proj):
    dp_count = lax.axis_size("dp")
    local_experts, block_hid, width = gate_proj.shape
    experts = local_experts * lax.axis_size("expert")
    token_count = tokens.shape[1]
    hid = local_experts * block_hid
    in_span = width // IN_CHUNKS
    out_span = width // OUT_CHUNKS
    batch = token_count // BATCHES
    half = batch // 2
    own = token_count // dp_count
    core_rows = 4 * batch

    bf16, f32 = jnp.bfloat16, jnp.float32
    vmem = pl.BlockSpec(memory_space=pltpu.VMEM)
    anywhere = pl.BlockSpec(memory_space=pl.ANY)
    dma = pltpu.SemaphoreType.DMA
    mixed = pl.pallas_call(
        functools.partial(fused, dp_count, local_experts),
        out_shape=jax.ShapeDtypeStruct((own, width), f32),
        in_specs=[vmem] * 4 + [anywhere] * 3,
        out_specs=vmem,
        scratch_shapes=[
            pltpu.VMEM((2 * hid, width), bf16),
            pltpu.VMEM((hid, width), bf16),
            pltpu.VMEM((IN_STEPS, 8, batch, in_span), bf16),
            pltpu.VMEM((in_span, 8 * batch), bf16),
            pltpu.VMEM((8, experts + 8, 128), f32),
            pltpu.VMEM((2, hid, 8 * batch), f32),
            pltpu.VMEM((8 * batch, hid), bf16),
            pltpu.VMEM((OUT_STEPS, core_rows, out_span), bf16),
            pltpu.VMEM((OUT_STEPS, core_rows, out_span), f32),
            pltpu.VMEM((OUT_STEPS, core_rows, out_span), bf16),
            pltpu.VMEM((OUT_STEPS, 2 * half, out_span), bf16),
            pltpu.VMEM((OUT_STEPS, 2 * half, out_span), bf16),
            pltpu.VMEM((OUT_STEPS, 2 * half, out_span), bf16),
            pltpu.VMEM((OUT_STEPS, 2 * half, out_span), bf16),
            pltpu.VMEM((OUT_STEPS, half, out_span), bf16),
            pltpu.VMEM((OUT_STEPS, half, out_span), bf16),
            pltpu.VMEM((OUT_STEPS, half, out_span), bf16),
            pltpu.VMEM((OUT_STEPS, half, out_span), bf16),
            pltpu.VMEM((OUT_STEPS, dp_count, own, out_span // BATCHES), f32),
            pltpu.VMEM((OUT_STEPS, dp_count, own, out_span // BATCHES), bf16),
            pltpu.VMEM((OUT_STEPS, dp_count - 1, own, out_span // BATCHES), bf16),
            dma((3,)),
            dma((7,)),
            dma((7,)),
            dma((IN_STEPS, 8)),
            dma((IN_STEPS, 8)),
            dma((OUT_STEPS, 4 + dp_count)),
            dma((OUT_STEPS, 4 + dp_count)),
        ],
        compiler_params=pltpu.CompilerParams(
            collective_id=0, has_side_effects=True, vmem_limit_bytes=56 * 1024 * 1024
        ),
        cost_estimate=pl.CostEstimate(
            flops=2 * 3 * 8 * token_count * hid * width,
            bytes_accessed=3 * hid * width * 2,
            transcendentals=8 * token_count * hid,
        ),
    )(
        tokens[0],
        norm_gain[None],
        expert_ids[0].T,
        route_weights[0].T,
        gate_proj.reshape(hid, width),
        up_proj.reshape(hid, width),
        down_proj.reshape(hid, width),
    )
    return mixed.astype(bf16)[None]


def rank_slots(id_table, expert_total):
    flat_ids = id_table.reshape(-1)
    onehot = (flat_ids[:, None] == jnp.arange(expert_total, dtype=jnp.int32)[None, :]).astype(
        jnp.int32
    )
    before = jnp.cumsum(onehot, axis=0) - onehot
    return jnp.sum(before * onehot, axis=1).reshape(id_table.shape)


def body(tokens, norm_gain, expert_ids, route_weights, gate_proj, up_proj, down_proj):
    dp_count = lax.axis_size("dp")
    expert_count = lax.axis_size("expert")
    local_experts = gate_proj.shape[0]
    model_width = tokens.shape[2]
    group_ids = expert_ids[0]
    group_weights = route_weights[0]
    group_size = group_ids.shape[0]
    own_rows = group_size // dp_count
    top_k = group_ids.shape[1]
    experts = local_experts * expert_count
    capacity = dp_count * (group_size * top_k // (experts * dp_count) + 1)
    tok_float = tokens[0].astype(jnp.float32)
    inv_rms = lax.rsqrt(jnp.mean(tok_float * tok_float, axis=-1, keepdims=True) + 1e-06)
    group_rows = (tok_float * inv_rms * norm_gain).astype(jnp.bfloat16)
    slot_rank = rank_slots(group_ids, experts)
    slot_index = group_ids * capacity + slot_rank
    token_order = jnp.broadcast_to(
        jnp.arange(group_size, dtype=jnp.int32)[:, None], (group_size, top_k)
    )
    sources = (
        jnp.full((experts * capacity,), group_size, jnp.int32)
        .at[slot_index.reshape(-1)]
        .set(token_order.reshape(-1))
    )
    padded = jnp.concatenate([group_rows, jnp.zeros((1, model_width), jnp.bfloat16)], axis=0)
    outgoing = jnp.take(padded, sources, axis=0).reshape(
        expert_count, local_experts, capacity, model_width
    )
    incoming = lax.all_to_all(outgoing, "expert", split_axis=0, concat_axis=0, tiled=True)
    gate_act = jnp.einsum("sjmd,jfd->sjmf", incoming, gate_proj, preferred_element_type=jnp.float32)
    up_act = jnp.einsum("sjmd,jfd->sjmf", incoming, up_proj, preferred_element_type=jnp.float32)
    hidden = (jax.nn.silu(gate_act) * up_act).astype(jnp.bfloat16)
    partial_rows = jnp.einsum(
        "sjmf,jfd->sjmd", hidden, down_proj, preferred_element_type=jnp.float32
    ).astype(jnp.bfloat16)
    returned = lax.all_to_all(partial_rows, "expert", split_axis=0, concat_axis=0, tiled=True)
    lookup = jnp.concatenate(
        [
            returned.reshape(experts * capacity, model_width),
            jnp.zeros((1, model_width), jnp.bfloat16),
        ],
        axis=0,
    )
    picked = (
        jnp.take(lookup, slot_index.reshape(-1), axis=0)
        .reshape(own_rows * lax.axis_size("dp"), top_k, model_width)
        .astype(jnp.float32)
    )
    mixed = lax.psum_scatter(
        jnp.sum(picked * group_weights[:, :, None], axis=1).astype(jnp.bfloat16),
        "dp",
        scatter_dimension=0,
        tiled=True,
    )
    return mixed[None]


def solution(mesh):
    placed = (
        P("expert", None, None),
        P(),
        P("expert", None, None),
        P("expert", None, None),
        P("expert", "dp", None),
        P("expert", "dp", None),
        P("expert", "dp", None),
    )
    small = mesh.shape["expert"] == 8 and mesh.shape["dp"] == 4
    return jax.shard_map(
        fused_body if small else body, mesh=mesh, in_specs=placed, out_specs=P("expert", "dp", None), check_vma=False
    )
```

```python
import functools

import jax
import jax.numpy as jnp
from jax import lax
from jax.experimental import pallas as pl
from jax.experimental.pallas import tpu as pltpu
from jax.sharding import PartitionSpec as P

MESH = pl.DeviceIdType.MESH
BATCHES = 2
IN_CHUNKS = 4
OUT_CHUNKS = 4
IN_STEPS = BATCHES * IN_CHUNKS
OUT_STEPS = BATCHES * OUT_CHUNKS
OWN, ALONG_X, ALONG_Y, DIAGONAL, SIBLING = 0, 1, 2, 3, 4


def fused(
    dp_count,
    local_experts,
    tok_ref,
    gain_ref,
    ids_ref,
    route_ref,
    gate_hbm,
    up_hbm,
    down_hbm,
    out_ref,
    w_in,
    w_out,
    rows,
    flipped,
    dense,
    acc,
    hidden,
    to_sib,
    kept,
    from_sib,
    to_x,
    to_y,
    from_x,
    from_y,
    to_x2,
    to_y2,
    from_x2,
    from_y2,
    summed,
    to_z,
    from_z,
    w_sem,
    d_send,
    d_recv,
    a_send,
    a_recv,
    r_send,
    r_recv,
):
    me = lax.axis_index("expert")
    plane = lax.axis_index("dp")
    sib = me + 1 - 2 * lax.rem(me, 2)
    nx = me + 2 - 4 * lax.rem(me // 2, 2)
    ny = me + 4 - 8 * (me // 4)
    token_count, width = tok_ref.shape
    in_span = width // IN_CHUNKS
    out_span = width // OUT_CHUNKS
    batch = token_count // BATCHES
    half = batch // 2
    own = token_count // dp_count
    piece = own // BATCHES
    hid = w_out.shape[0]
    all_rows = 8 * batch
    core_rows = 4 * batch

    loads = [
        pltpu.make_async_copy(gate_hbm, w_in.at[pl.ds(0, hid)], w_sem.at[0]),
        pltpu.make_async_copy(up_hbm, w_in.at[pl.ds(hid, hid)], w_sem.at[1]),
        pltpu.make_async_copy(down_hbm, w_out, w_sem.at[2]),
    ]
    for load in loads:
        load.start()

    barrier = pltpu.get_barrier_semaphore()
    for peer in (sib, nx, ny):
        pl.semaphore_signal(barrier, inc=1, device_id={"expert": peer}, device_id_type=MESH)
    for step in range(1, dp_count):
        pl.semaphore_signal(
            barrier,
            inc=1,
            device_id={"dp": lax.rem(plane + step, dp_count)},
            device_id_type=MESH,
        )

    for c in range(IN_CHUNKS):
        cols = slice(c * in_span, (c + 1) * in_span)
        part = tok_ref[:, cols].astype(jnp.float32) * gain_ref[:, cols]
        for b in range(BATCHES):
            picked = [
                part[z * own + b * piece : z * own + (b + 1) * piece] for z in range(dp_count)
            ]
            rows[b * IN_CHUNKS + c, OWN] = jnp.concatenate(picked, axis=0).astype(jnp.bfloat16)
    pl.semaphore_wait(barrier, 3 + dp_count - 1)

    def push(src, dst, send, recv, **where):
        return pltpu.make_async_remote_copy(
            src_ref=src,
            dst_ref=dst,
            send_sem=send,
            recv_sem=recv,
            device_id=where,
            device_id_type=MESH,
        )

    def dense_push(k, src, dst, peer):
        return push(dense.at[src], dense.at[dst], d_send.at[k], d_recv.at[k], expert=peer)

    dense_copies = [
        dense_push(0, OWN, ALONG_X, nx),
        dense_push(1, OWN, ALONG_Y, ny),
        dense_push(2, OWN, SIBLING, sib),
        dense_push(3, ALONG_X, DIAGONAL, ny),
        dense_push(4, ALONG_X, SIBLING + ALONG_X, sib),
        dense_push(5, ALONG_Y, SIBLING + ALONG_Y, sib),
        dense_push(6, DIAGONAL, SIBLING + DIAGONAL, sib),
    ]

    def gather_copies(c):
        def go(k, src, dst, peer, part=None):
            a, b = rows.at[c, src], rows.at[c, dst]
            if part is not None:
                a = rows.at[c, src, pl.ds(part * half, half)]
                b = rows.at[c, dst, pl.ds(part * half, half)]
            return push(a, b, a_send.at[c, k], a_recv.at[c, k], expert=peer)

        return [
            go(0, OWN, ALONG_X, nx),
            go(1, OWN, ALONG_Y, ny),
            go(2, OWN, SIBLING, sib),
            go(3, ALONG_X, DIAGONAL, ny, 0),
            go(4, ALONG_Y, DIAGONAL, nx, 1),
            go(5, ALONG_X, SIBLING + ALONG_X, sib),
            go(6, ALONG_Y, SIBLING + ALONG_Y, sib),
            go(7, DIAGONAL, SIBLING + DIAGONAL, sib),
        ]

    gather = [gather_copies(s) for s in range(IN_STEPS)]

    def share(s):
        for k in range(3):
            gather[s][k].start()

    for s in range(IN_CHUNKS):
        share(s)

    tok = tok_ref[...].astype(jnp.float32)
    inv_rms = lax.rsqrt(jnp.mean(tok * tok, axis=-1, keepdims=True) + 1e-06)
    token = lax.broadcasted_iota(jnp.int32, (token_count, 128), 0)
    lane = lax.broadcasted_iota(jnp.int32, (token_count, 128), 1)
    within = lax.rem(token, own)
    ordered = lane == (within // piece) * batch + (token // own) * piece + lax.rem(within, piece)
    experts = dense.shape[1] - 8

    def regroup(by_choice):
        starts = [z * own + b * piece for b in range(BATCHES) for z in range(dp_count)]
        return jnp.concatenate([by_choice[:, at : at + piece] for at in starts], axis=1)

    ids, route = regroup(ids_ref[...]), regroup(route_ref[...])
    table = [
        jnp.sum(jnp.where(ids == e, route, 0.0), axis=0, keepdims=True) for e in range(experts)
    ]
    dense[OWN] = jnp.zeros(dense.shape[1:], dense.dtype)
    dense[OWN, :experts, :token_count] = jnp.concatenate(table, axis=0)
    inv_row = jnp.sum(jnp.where(ordered, inv_rms, 0.0), axis=0, keepdims=True)
    dense[OWN, experts:] = jnp.broadcast_to(inv_row, (8, 128))
    for k in range(3):
        dense_copies[k].start()

    def forward(c):
        gather[c][0].wait_recv()
        gather[c][3].start()
        gather[c][5].start()
        gather[c][1].wait_recv()
        gather[c][4].start()
        gather[c][6].start()

    def forward_diagonal(c):
        gather[c][3].wait_recv()
        gather[c][4].wait_recv()
        gather[c][7].start()

    def multiply_in(s):
        c = s % IN_CHUNKS
        for k in (2, 5, 6, 7):
            gather[s][k].wait_recv()
        flipped[...] = rows[s].reshape(all_rows, in_span).T

        @pl.loop(0, 2)
        def _(t):
            w = w_in[
                pl.ds(pl.multiple_of(t * hid, hid), hid), c * in_span : (c + 1) * in_span
            ]
            y = jnp.dot(w, flipped[...], preferred_element_type=jnp.float32)
            if c == 0:
                acc[t] = y
            else:
                acc[t] += y

    expert_rows = lax.broadcasted_iota(jnp.int32, dense.shape[1:], 0)
    per_expert = hid // local_experts

    def batch_row(b, row):
        picked = [
            jnp.sum(jnp.where(expert_rows == row, dense[p], 0.0), axis=0, keepdims=True)
            for p in range(8)
        ]
        return jnp.concatenate([r[:, b * batch : (b + 1) * batch] for r in picked], axis=1)

    def activate(b):
        inv = batch_row(b, experts)
        for j in range(local_experts):
            scale = inv * batch_row(b, me * local_experts + j)
            for k in range(j * per_expert, (j + 1) * per_expert, 128):
                g = acc[0, k : k + 128] * inv
                h = g / (1.0 + jnp.exp(-g)) * (acc[1, k : k + 128] * scale)
                hidden[:, k : k + 128] = h.astype(jnp.bfloat16).T

    def reduce_copies(n):
        def go(k, src, dst, **where):
            return push(src, dst, r_send.at[n, k], r_recv.at[n, k], **where)

        copies = [
            go(0, to_sib.at[n], from_sib.at[n], expert=sib),
            go(1, to_x.at[n], from_x.at[n], expert=nx),
            go(2, to_y.at[n], from_y.at[n], expert=ny),
            go(3, to_y2.at[n], from_y2.at[n], expert=ny),
            go(4, to_x2.at[n], from_x2.at[n], expert=nx),
        ]
        for step in range(1, dp_count):
            peer = lax.rem(plane + step, dp_count)
            copies.append(go(4 + step, to_z.at[n, peer], from_z.at[n, step - 1], dp=peer))
        return copies

    reduce = [reduce_copies(n) for n in range(OUT_STEPS)]

    def multiply_out(n):
        step = 512

        @pl.loop(0, out_span // step)
        def _(t):
            w = w_out[:, pl.ds(pl.multiple_of(n % OUT_CHUNKS * out_span + t * step, step), step)]
            y = jnp.dot(hidden[...], w, preferred_element_type=jnp.float32)
            cols = pl.ds(pl.multiple_of(t * step, step), step)
            to_sib[n, :, cols] = y[core_rows:].astype(jnp.bfloat16)
            kept[n, :, cols] = y[:core_rows]

        reduce[n][0].start()

    def block(place, part):
        return slice(place * batch + part * half, place * batch + (part + 1) * half)

    def pair_sum(n):
        reduce[n][0].wait_recv()

        def total(place, part):
            at = block(place, part)
            return kept[n, at] + from_sib[n, at].astype(jnp.float32)

        to_x[n, :half] = total(ALONG_X, 0).astype(jnp.bfloat16)
        to_x[n, half:] = total(DIAGONAL, 0).astype(jnp.bfloat16)
        reduce[n][1].start()
        to_y[n, :half] = total(ALONG_Y, 1).astype(jnp.bfloat16)
        to_y[n, half:] = total(DIAGONAL, 1).astype(jnp.bfloat16)
        reduce[n][2].start()
        for place, part in ((OWN, 0), (OWN, 1), (ALONG_Y, 0), (ALONG_X, 1)):
            kept[n, block(place, part)] = total(place, part)

    def second_hop(n):
        reduce[n][1].wait_recv()
        to_y2[n] = (
            kept[n, block(ALONG_Y, 0)] + from_x[n, half:].astype(jnp.float32)
        ).astype(jnp.bfloat16)
        reduce[n][3].start()
        reduce[n][2].wait_recv()
        to_x2[n] = (
            kept[n, block(ALONG_X, 1)] + from_y[n, half:].astype(jnp.float32)
        ).astype(jnp.bfloat16)
        reduce[n][4].start()

    def across_planes(n):
        reduce[n][3].wait_recv()
        reduce[n][4].wait_recv()
        first = (
            kept[n, block(OWN, 0)]
            + from_x[n, :half].astype(jnp.float32)
            + from_y2[n].astype(jnp.float32)
        )
        second = (
            kept[n, block(OWN, 1)]
            + from_y[n, :half].astype(jnp.float32)
            + from_x2[n].astype(jnp.float32)
        )
        per_half = half // piece
        for i in range(dp_count):
            source = first if i < per_half else second
            at = i % per_half * piece
            rows_i = source[at : at + piece]
            folded = jnp.concatenate(
                [rows_i[:, f * fold : (f + 1) * fold] for f in range(BATCHES)], axis=0
            )
            summed[n, i] = folded
            to_z[n, i] = folded.astype(jnp.bfloat16)
        for step in range(1, dp_count):
            reduce[n][4 + step].start()

    fold = out_span // BATCHES

    def finish(n):
        total = summed[n, plane]
        for step in range(1, dp_count):
            reduce[n][4 + step].wait_recv()
            total = total + from_z[n, step - 1].astype(jnp.float32)
        b, c = n // OUT_CHUNKS, n % OUT_CHUNKS
        for f in range(BATCHES):
            at = c * out_span + f * fold
            out_ref[b * piece : (b + 1) * piece, at : at + fold] = total[
                f * piece : (f + 1) * piece
            ]

    forward(0)
    share(4)
    forward(1)
    share(5)
    dense_copies[0].wait_recv()
    dense_copies[3].start()
    dense_copies[4].start()
    dense_copies[1].wait_recv()
    dense_copies[5].start()
    forward_diagonal(0)
    forward(2)
    share(6)
    forward_diagonal(1)
    dense_copies[3].wait_recv()
    dense_copies[6].start()
    loads[0].wait()
    loads[1].wait()
    multiply_in(0)
    forward(3)
    share(7)
    forward_diagonal(2)
    multiply_in(1)
    forward_diagonal(3)
    multiply_in(2)
    forward(4)
    multiply_in(3)
    for k in (2, 4, 5, 6):
        dense_copies[k].wait_recv()
    activate(0)
    loads[2].wait()
    multiply_out(0)
    forward(5)
    forward_diagonal(4)
    multiply_out(1)
    forward(6)
    forward_diagonal(5)
    multiply_out(2)
    pair_sum(0)
    forward(7)
    forward_diagonal(6)
    multiply_out(3)
    pair_sum(1)
    multiply_in(4)
    pair_sum(2)
    multiply_in(5)
    forward_diagonal(7)
    pair_sum(3)
    multiply_in(6)
    multiply_in(7)
    second_hop(0)
    second_hop(1)
    activate(1)
    multiply_out(4)
    second_hop(2)
    multiply_out(5)
    pair_sum(4)
    second_hop(3)
    multiply_out(6)
    pair_sum(5)
    across_planes(0)
    multiply_out(7)
    pair_sum(6)
    across_planes(1)
    pair_sum(7)
    across_planes(2)
    across_planes(3)
    second_hop(4)
    finish(0)
    second_hop(5)
    finish(1)
    across_planes(4)
    second_hop(6)
    finish(2)
    across_planes(5)
    second_hop(7)
    finish(3)
    across_planes(6)
    finish(4)
    across_planes(7)
    finish(5)
    finish(6)
    finish(7)

    for copy in dense_copies:
        copy.wait_send()
    for copies in gather + reduce:
        for copy in copies:
            copy.wait_send()


def fused_body(tokens, norm_gain, expert_ids, route_weights, gate_proj, up_proj, down_proj):
    dp_count = lax.axis_size("dp")
    local_experts, block_hid, width = gate_proj.shape
    experts = local_experts * lax.axis_size("expert")
    token_count = tokens.shape[1]
    hid = local_experts * block_hid
    in_span = width // IN_CHUNKS
    out_span = width // OUT_CHUNKS
    batch = token_count // BATCHES
    half = batch // 2
    own = token_count // dp_count
    core_rows = 4 * batch

    bf16, f32 = jnp.bfloat16, jnp.float32
    vmem = pl.BlockSpec(memory_space=pltpu.VMEM)
    anywhere = pl.BlockSpec(memory_space=pl.ANY)
    dma = pltpu.SemaphoreType.DMA
    mixed = pl.pallas_call(
        functools.partial(fused, dp_count, local_experts),
        out_shape=jax.ShapeDtypeStruct((own, width), f32),
        in_specs=[vmem] * 4 + [anywhere] * 3,
        out_specs=vmem,
        scratch_shapes=[
            pltpu.VMEM((2 * hid, width), bf16),
            pltpu.VMEM((hid, width), bf16),
            pltpu.VMEM((IN_STEPS, 8, batch, in_span), bf16),
            pltpu.VMEM((in_span, 8 * batch), bf16),
            pltpu.VMEM((8, experts + 8, 128), f32),
            pltpu.VMEM((2, hid, 8 * batch), f32),
            pltpu.VMEM((8 * batch, hid), bf16),
            pltpu.VMEM((OUT_STEPS, core_rows, out_span), bf16),
            pltpu.VMEM((OUT_STEPS, core_rows, out_span), f32),
            pltpu.VMEM((OUT_STEPS, core_rows, out_span), bf16),
            pltpu.VMEM((OUT_STEPS, 2 * half, out_span), bf16),
            pltpu.VMEM((OUT_STEPS, 2 * half, out_span), bf16),
            pltpu.VMEM((OUT_STEPS, 2 * half, out_span), bf16),
            pltpu.VMEM((OUT_STEPS, 2 * half, out_span), bf16),
            pltpu.VMEM((OUT_STEPS, half, out_span), bf16),
            pltpu.VMEM((OUT_STEPS, half, out_span), bf16),
            pltpu.VMEM((OUT_STEPS, half, out_span), bf16),
            pltpu.VMEM((OUT_STEPS, half, out_span), bf16),
            pltpu.VMEM((OUT_STEPS, dp_count, own, out_span // BATCHES), f32),
            pltpu.VMEM((OUT_STEPS, dp_count, own, out_span // BATCHES), bf16),
            pltpu.VMEM((OUT_STEPS, dp_count - 1, own, out_span // BATCHES), bf16),
            dma((3,)),
            dma((7,)),
            dma((7,)),
            dma((IN_STEPS, 8)),
            dma((IN_STEPS, 8)),
            dma((OUT_STEPS, 4 + dp_count)),
            dma((OUT_STEPS, 4 + dp_count)),
        ],
        compiler_params=pltpu.CompilerParams(
            collective_id=0, has_side_effects=True, vmem_limit_bytes=56 * 1024 * 1024
        ),
        cost_estimate=pl.CostEstimate(
            flops=2 * 3 * 8 * token_count * hid * width,
            bytes_accessed=3 * hid * width * 2,
            transcendentals=8 * token_count * hid,
        ),
    )(
        tokens[0],
        norm_gain[None],
        expert_ids[0].T,
        route_weights[0].T,
        gate_proj.reshape(hid, width),
        up_proj.reshape(hid, width),
        down_proj.reshape(hid, width),
    )
    return mixed.astype(bf16)[None]


def rank_slots(id_table, expert_total):
    flat_ids = id_table.reshape(-1)
    onehot = (flat_ids[:, None] == jnp.arange(expert_total, dtype=jnp.int32)[None, :]).astype(
        jnp.int32
    )
    before = jnp.cumsum(onehot, axis=0) - onehot
    return jnp.sum(before * onehot, axis=1).reshape(id_table.shape)


def body(tokens, norm_gain, expert_ids, route_weights, gate_proj, up_proj, down_proj):
    dp_count = lax.axis_size("dp")
    expert_count = lax.axis_size("expert")
    local_experts = gate_proj.shape[0]
    model_width = tokens.shape[2]
    group_ids = expert_ids[0]
    group_weights = route_weights[0]
    group_size = group_ids.shape[0]
    own_rows = group_size // dp_count
    top_k = group_ids.shape[1]
    experts = local_experts * expert_count
    capacity = dp_count * (group_size * top_k // (experts * dp_count) + 1)
    tok_float = tokens[0].astype(jnp.float32)
    inv_rms = lax.rsqrt(jnp.mean(tok_float * tok_float, axis=-1, keepdims=True) + 1e-06)
    group_rows = (tok_float * inv_rms * norm_gain).astype(jnp.bfloat16)
    slot_rank = rank_slots(group_ids, experts)
    slot_index = group_ids * capacity + slot_rank
    token_order = jnp.broadcast_to(
        jnp.arange(group_size, dtype=jnp.int32)[:, None], (group_size, top_k)
    )
    sources = (
        jnp.full((experts * capacity,), group_size, jnp.int32)
        .at[slot_index.reshape(-1)]
        .set(token_order.reshape(-1))
    )
    padded = jnp.concatenate([group_rows, jnp.zeros((1, model_width), jnp.bfloat16)], axis=0)
    outgoing = jnp.take(padded, sources, axis=0).reshape(
        expert_count, local_experts, capacity, model_width
    )
    incoming = lax.all_to_all(outgoing, "expert", split_axis=0, concat_axis=0, tiled=True)
    gate_act = jnp.einsum("sjmd,jfd->sjmf", incoming, gate_proj, preferred_element_type=jnp.float32)
    up_act = jnp.einsum("sjmd,jfd->sjmf", incoming, up_proj, preferred_element_type=jnp.float32)
    hidden = (jax.nn.silu(gate_act) * up_act).astype(jnp.bfloat16)
    partial_rows = jnp.einsum(
        "sjmf,jfd->sjmd", hidden, down_proj, preferred_element_type=jnp.float32
    ).astype(jnp.bfloat16)
    returned = lax.all_to_all(partial_rows, "expert", split_axis=0, concat_axis=0, tiled=True)
    lookup = jnp.concatenate(
        [
            returned.reshape(experts * capacity, model_width),
            jnp.zeros((1, model_width), jnp.bfloat16),
        ],
        axis=0,
    )
    picked = (
        jnp.take(lookup, slot_index.reshape(-1), axis=0)
        .reshape(own_rows * lax.axis_size("dp"), top_k, model_width)
        .astype(jnp.float32)
    )
    mixed = lax.psum_scatter(
        jnp.sum(picked * group_weights[:, :, None], axis=1).astype(jnp.bfloat16),
        "dp",
        scatter_dimension=0,
        tiled=True,
    )
    return mixed[None]


def solution(mesh):
    placed = (
        P("expert", None, None),
        P(),
        P("expert", None, None),
        P("expert", None, None),
        P("expert", "dp", None),
        P("expert", "dp", None),
        P("expert", "dp", None),
    )
    small = mesh.shape["expert"] == 8 and mesh.shape["dp"] == 4
    return jax.shard_map(
        fused_body if small else body, mesh=mesh, in_specs=placed, out_specs=P("expert", "dp", None), check_vma=False
    )
```

```python
import functools

import jax
import jax.numpy as jnp
from jax import lax
from jax.experimental import pallas as pl
from jax.experimental.pallas import tpu as pltpu
from jax.sharding import PartitionSpec as P

MESH = pl.DeviceIdType.MESH
BATCHES = 2
IN_CHUNKS = 2
OUT_CHUNKS = 4
IN_STEPS = BATCHES * IN_CHUNKS
OUT_STEPS = BATCHES * OUT_CHUNKS
OWN, ALONG_X, ALONG_Y, DIAGONAL, SIBLING = 0, 1, 2, 3, 4


def fused(
    dp_count,
    local_experts,
    tok_ref,
    gain_ref,
    ids_ref,
    route_ref,
    gate_hbm,
    up_hbm,
    down_hbm,
    out_ref,
    w_in,
    w_out,
    rows,
    flipped,
    dense,
    acc,
    hidden,
    to_sib,
    kept,
    from_sib,
    to_x,
    to_y,
    from_x,
    from_y,
    to_x2,
    to_y2,
    from_x2,
    from_y2,
    summed,
    to_z,
    from_z,
    w_sem,
    d_send,
    d_recv,
    a_send,
    a_recv,
    r_send,
    r_recv,
):
    me = lax.axis_index("expert")
    plane = lax.axis_index("dp")
    sib = me + 1 - 2 * lax.rem(me, 2)
    nx = me + 2 - 4 * lax.rem(me // 2, 2)
    ny = me + 4 - 8 * (me // 4)
    token_count, width = tok_ref.shape
    in_span = width // IN_CHUNKS
    out_span = width // OUT_CHUNKS
    batch = token_count // BATCHES
    half = batch // 2
    own = token_count // dp_count
    piece = own // BATCHES
    hid = w_out.shape[0]
    all_rows = 8 * batch
    core_rows = 4 * batch

    loads = [
        pltpu.make_async_copy(gate_hbm, w_in.at[pl.ds(0, hid)], w_sem.at[0]),
        pltpu.make_async_copy(up_hbm, w_in.at[pl.ds(hid, hid)], w_sem.at[1]),
        pltpu.make_async_copy(down_hbm, w_out, w_sem.at[2]),
    ]
    for load in loads:
        load.start()

    barrier = pltpu.get_barrier_semaphore()
    for peer in (sib, nx, ny):
        pl.semaphore_signal(barrier, inc=1, device_id={"expert": peer}, device_id_type=MESH)
    for step in range(1, dp_count):
        pl.semaphore_signal(
            barrier,
            inc=1,
            device_id={"dp": lax.rem(plane + step, dp_count)},
            device_id_type=MESH,
        )

    for c in range(IN_CHUNKS):
        cols = slice(c * in_span, (c + 1) * in_span)
        part = tok_ref[:, cols].astype(jnp.float32) * gain_ref[:, cols]
        for b in range(BATCHES):
            picked = [
                part[z * own + b * piece : z * own + (b + 1) * piece] for z in range(dp_count)
            ]
            rows[b * IN_CHUNKS + c, OWN] = jnp.concatenate(picked, axis=0).astype(jnp.bfloat16)
    pl.semaphore_wait(barrier, 3 + dp_count - 1)

    def push(src, dst, send, recv, **where):
        return pltpu.make_async_remote_copy(
            src_ref=src,
            dst_ref=dst,
            send_sem=send,
            recv_sem=recv,
            device_id=where,
            device_id_type=MESH,
        )

    def dense_push(k, src, dst, peer):
        return push(dense.at[src], dense.at[dst], d_send.at[k], d_recv.at[k], expert=peer)

    dense_copies = [
        dense_push(0, OWN, ALONG_X, nx),
        dense_push(1, OWN, ALONG_Y, ny),
        dense_push(2, OWN, SIBLING, sib),
        dense_push(3, ALONG_X, DIAGONAL, ny),
        dense_push(4, ALONG_X, SIBLING + ALONG_X, sib),
        dense_push(5, ALONG_Y, SIBLING + ALONG_Y, sib),
        dense_push(6, DIAGONAL, SIBLING + DIAGONAL, sib),
    ]

    def gather_copies(c):
        def go(k, src, dst, peer, part=None):
            a, b = rows.at[c, src], rows.at[c, dst]
            if part is not None:
                a = rows.at[c, src, pl.ds(part * half, half)]
                b = rows.at[c, dst, pl.ds(part * half, half)]
            return push(a, b, a_send.at[c, k], a_recv.at[c, k], expert=peer)

        return [
            go(0, OWN, ALONG_X, nx),
            go(1, OWN, ALONG_Y, ny),
            go(2, OWN, SIBLING, sib),
            go(3, ALONG_X, DIAGONAL, ny, 0),
            go(4, ALONG_Y, DIAGONAL, nx, 1),
            go(5, ALONG_X, SIBLING + ALONG_X, sib),
            go(6, ALONG_Y, SIBLING + ALONG_Y, sib),
            go(7, DIAGONAL, SIBLING + DIAGONAL, sib),
        ]

    gather = [gather_copies(s) for s in range(IN_STEPS)]

    def share(s):
        for k in range(3):
            gather[s][k].start()

    share(0)
    share(1)

    tok = tok_ref[...].astype(jnp.float32)
    inv_rms = lax.rsqrt(jnp.mean(tok * tok, axis=-1, keepdims=True) + 1e-06)
    token = lax.broadcasted_iota(jnp.int32, (token_count, 128), 0)
    lane = lax.broadcasted_iota(jnp.int32, (token_count, 128), 1)
    within = lax.rem(token, own)
    ordered = lane == (within // piece) * batch + (token // own) * piece + lax.rem(within, piece)
    experts = dense.shape[1] - 8

    def regroup(by_choice):
        starts = [z * own + b * piece for b in range(BATCHES) for z in range(dp_count)]
        return jnp.concatenate([by_choice[:, at : at + piece] for at in starts], axis=1)

    ids, route = regroup(ids_ref[...]), regroup(route_ref[...])
    table = [
        jnp.sum(jnp.where(ids == e, route, 0.0), axis=0, keepdims=True) for e in range(experts)
    ]
    dense[OWN] = jnp.zeros(dense.shape[1:], dense.dtype)
    dense[OWN, :experts, :token_count] = jnp.concatenate(table, axis=0)
    inv_row = jnp.sum(jnp.where(ordered, inv_rms, 0.0), axis=0, keepdims=True)
    dense[OWN, experts:] = jnp.broadcast_to(inv_row, (8, 128))
    for k in range(3):
        dense_copies[k].start()

    def forward(c):
        gather[c][0].wait_recv()
        gather[c][3].start()
        gather[c][5].start()
        gather[c][1].wait_recv()
        gather[c][4].start()
        gather[c][6].start()

    def forward_diagonal(c):
        gather[c][3].wait_recv()
        gather[c][4].wait_recv()
        gather[c][7].start()

    def multiply_in(s):
        c = s % IN_CHUNKS
        for k in (2, 5, 6, 7):
            gather[s][k].wait_recv()
        flipped[...] = rows[s].reshape(all_rows, in_span).T

        @pl.loop(0, 2)
        def _(t):
            w = w_in[
                pl.ds(pl.multiple_of(t * hid, hid), hid), c * in_span : (c + 1) * in_span
            ]
            y = jnp.dot(w, flipped[...], preferred_element_type=jnp.float32)
            if c == 0:
                acc[t] = y
            else:
                acc[t] += y

    expert_rows = lax.broadcasted_iota(jnp.int32, dense.shape[1:], 0)
    per_expert = hid // local_experts

    def batch_row(b, row):
        picked = [
            jnp.sum(jnp.where(expert_rows == row, dense[p], 0.0), axis=0, keepdims=True)
            for p in range(8)
        ]
        return jnp.concatenate([r[:, b * batch : (b + 1) * batch] for r in picked], axis=1)

    def activate(b):
        inv = batch_row(b, experts)
        for j in range(local_experts):
            scale = inv * batch_row(b, me * local_experts + j)
            for k in range(j * per_expert, (j + 1) * per_expert, 128):
                g = acc[0, k : k + 128] * inv
                h = g / (1.0 + jnp.exp(-g)) * (acc[1, k : k + 128] * scale)
                hidden[:, k : k + 128] = h.astype(jnp.bfloat16).T

    def reduce_copies(n):
        def go(k, src, dst, **where):
            return push(src, dst, r_send.at[n, k], r_recv.at[n, k], **where)

        copies = [
            go(0, to_sib.at[n], from_sib.at[n], expert=sib),
            go(1, to_x.at[n], from_x.at[n], expert=nx),
            go(2, to_y.at[n], from_y.at[n], expert=ny),
            go(3, to_y2.at[n], from_y2.at[n], expert=ny),
            go(4, to_x2.at[n], from_x2.at[n], expert=nx),
        ]
        for step in range(1, dp_count):
            peer = lax.rem(plane + step, dp_count)
            copies.append(go(4 + step, to_z.at[n, peer], from_z.at[n, step - 1], dp=peer))
        return copies

    reduce = [reduce_copies(n) for n in range(OUT_STEPS)]

    def multiply_out(n):
        step = 512

        @pl.loop(0, out_span // step)
        def _(t):
            w = w_out[:, pl.ds(pl.multiple_of(n % OUT_CHUNKS * out_span + t * step, step), step)]
            y = jnp.dot(hidden[...], w, preferred_element_type=jnp.float32)
            cols = pl.ds(pl.multiple_of(t * step, step), step)
            to_sib[n, :, cols] = y[core_rows:].astype(jnp.bfloat16)
            kept[n, :, cols] = y[:core_rows]

        reduce[n][0].start()

    def block(place, part):
        return slice(place * batch + part * half, place * batch + (part + 1) * half)

    def pair_sum(n):
        reduce[n][0].wait_recv()

        def total(place, part):
            at = block(place, part)
            return kept[n, at] + from_sib[n, at].astype(jnp.float32)

        to_x[n, :half] = total(ALONG_X, 0).astype(jnp.bfloat16)
        to_x[n, half:] = total(DIAGONAL, 0).astype(jnp.bfloat16)
        reduce[n][1].start()
        to_y[n, :half] = total(ALONG_Y, 1).astype(jnp.bfloat16)
        to_y[n, half:] = total(DIAGONAL, 1).astype(jnp.bfloat16)
        reduce[n][2].start()
        for place, part in ((OWN, 0), (OWN, 1), (ALONG_Y, 0), (ALONG_X, 1)):
            kept[n, block(place, part)] = total(place, part)

    def second_hop(n):
        reduce[n][1].wait_recv()
        to_y2[n] = (
            kept[n, block(ALONG_Y, 0)] + from_x[n, half:].astype(jnp.float32)
        ).astype(jnp.bfloat16)
        reduce[n][3].start()
        reduce[n][2].wait_recv()
        to_x2[n] = (
            kept[n, block(ALONG_X, 1)] + from_y[n, half:].astype(jnp.float32)
        ).astype(jnp.bfloat16)
        reduce[n][4].start()

    def across_planes(n):
        reduce[n][3].wait_recv()
        reduce[n][4].wait_recv()
        first = (
            kept[n, block(OWN, 0)]
            + from_x[n, :half].astype(jnp.float32)
            + from_y2[n].astype(jnp.float32)
        )
        second = (
            kept[n, block(OWN, 1)]
            + from_y[n, :half].astype(jnp.float32)
            + from_x2[n].astype(jnp.float32)
        )
        per_half = half // piece
        for i in range(dp_count):
            source = first if i < per_half else second
            at = i % per_half * piece
            rows_i = source[at : at + piece]
            folded = jnp.concatenate(
                [rows_i[:, f * fold : (f + 1) * fold] for f in range(BATCHES)], axis=0
            )
            summed[n, i] = folded
            to_z[n, i] = folded.astype(jnp.bfloat16)
        for step in range(1, dp_count):
            reduce[n][4 + step].start()

    fold = out_span // BATCHES

    def finish(n):
        total = summed[n, plane]
        for step in range(1, dp_count):
            reduce[n][4 + step].wait_recv()
            total = total + from_z[n, step - 1].astype(jnp.float32)
        b, c = n // OUT_CHUNKS, n % OUT_CHUNKS
        for f in range(BATCHES):
            at = c * out_span + f * fold
            out_ref[b * piece : (b + 1) * piece, at : at + fold] = total[
                f * piece : (f + 1) * piece
            ]

    forward(0)
    share(2)
    dense_copies[0].wait_recv()
    dense_copies[3].start()
    dense_copies[4].start()
    dense_copies[1].wait_recv()
    dense_copies[5].start()
    forward(1)
    share(3)
    forward_diagonal(0)
    dense_copies[3].wait_recv()
    dense_copies[6].start()
    loads[0].wait()
    loads[1].wait()
    multiply_in(0)
    forward_diagonal(1)
    forward(2)
    multiply_in(1)
    for k in (2, 4, 5, 6):
        dense_copies[k].wait_recv()
    activate(0)
    loads[2].wait()
    multiply_out(0)
    multiply_out(1)
    forward(3)
    multiply_out(2)
    pair_sum(0)
    multiply_out(3)
    pair_sum(1)
    forward_diagonal(2)
    multiply_in(2)
    pair_sum(2)
    pair_sum(3)
    forward_diagonal(3)
    multiply_in(3)
    activate(1)
    multiply_out(4)
    multiply_out(5)
    pair_sum(4)
    second_hop(0)
    multiply_out(6)
    pair_sum(5)
    second_hop(1)
    multiply_out(7)
    pair_sum(6)
    second_hop(2)
    pair_sum(7)
    second_hop(3)
    across_planes(0)
    across_planes(1)
    across_planes(2)
    across_planes(3)
    second_hop(4)
    finish(0)
    second_hop(5)
    finish(1)
    across_planes(4)
    second_hop(6)
    finish(2)
    across_planes(5)
    second_hop(7)
    finish(3)
    across_planes(6)
    finish(4)
    across_planes(7)
    finish(5)
    finish(6)
    finish(7)

    for copy in dense_copies:
        copy.wait_send()
    for copies in gather + reduce:
        for copy in copies:
            copy.wait_send()


def fused_body(tokens, norm_gain, expert_ids, route_weights, gate_proj, up_proj, down_proj):
    dp_count = lax.axis_size("dp")
    local_experts, block_hid, width = gate_proj.shape
    experts = local_experts * lax.axis_size("expert")
    token_count = tokens.shape[1]
    hid = local_experts * block_hid
    in_span = width // IN_CHUNKS
    out_span = width // OUT_CHUNKS
    batch = token_count // BATCHES
    half = batch // 2
    own = token_count // dp_count
    core_rows = 4 * batch

    bf16, f32 = jnp.bfloat16, jnp.float32
    vmem = pl.BlockSpec(memory_space=pltpu.VMEM)
    anywhere = pl.BlockSpec(memory_space=pl.ANY)
    dma = pltpu.SemaphoreType.DMA
    mixed = pl.pallas_call(
        functools.partial(fused, dp_count, local_experts),
        out_shape=jax.ShapeDtypeStruct((own, width), f32),
        in_specs=[vmem] * 4 + [anywhere] * 3,
        out_specs=vmem,
        scratch_shapes=[
            pltpu.VMEM((2 * hid, width), bf16),
            pltpu.VMEM((hid, width), bf16),
            pltpu.VMEM((IN_STEPS, 8, batch, in_span), bf16),
            pltpu.VMEM((in_span, 8 * batch), bf16),
            pltpu.VMEM((8, experts + 8, 128), f32),
            pltpu.VMEM((2, hid, 8 * batch), f32),
            pltpu.VMEM((8 * batch, hid), bf16),
            pltpu.VMEM((OUT_STEPS, core_rows, out_span), bf16),
            pltpu.VMEM((OUT_STEPS, core_rows, out_span), f32),
            pltpu.VMEM((OUT_STEPS, core_rows, out_span), bf16),
            pltpu.VMEM((OUT_STEPS, 2 * half, out_span), bf16),
            pltpu.VMEM((OUT_STEPS, 2 * half, out_span), bf16),
            pltpu.VMEM((OUT_STEPS, 2 * half, out_span), bf16),
            pltpu.VMEM((OUT_STEPS, 2 * half, out_span), bf16),
            pltpu.VMEM((OUT_STEPS, half, out_span), bf16),
            pltpu.VMEM((OUT_STEPS, half, out_span), bf16),
            pltpu.VMEM((OUT_STEPS, half, out_span), bf16),
            pltpu.VMEM((OUT_STEPS, half, out_span), bf16),
            pltpu.VMEM((OUT_STEPS, dp_count, own, out_span // BATCHES), f32),
            pltpu.VMEM((OUT_STEPS, dp_count, own, out_span // BATCHES), bf16),
            pltpu.VMEM((OUT_STEPS, dp_count - 1, own, out_span // BATCHES), bf16),
            dma((3,)),
            dma((7,)),
            dma((7,)),
            dma((IN_STEPS, 8)),
            dma((IN_STEPS, 8)),
            dma((OUT_STEPS, 4 + dp_count)),
            dma((OUT_STEPS, 4 + dp_count)),
        ],
        compiler_params=pltpu.CompilerParams(
            collective_id=0, has_side_effects=True, vmem_limit_bytes=56 * 1024 * 1024
        ),
        cost_estimate=pl.CostEstimate(
            flops=2 * 3 * 8 * token_count * hid * width,
            bytes_accessed=3 * hid * width * 2,
            transcendentals=8 * token_count * hid,
        ),
    )(
        tokens[0],
        norm_gain[None],
        expert_ids[0].T,
        route_weights[0].T,
        gate_proj.reshape(hid, width),
        up_proj.reshape(hid, width),
        down_proj.reshape(hid, width),
    )
    return mixed.astype(bf16)[None]


def rank_slots(id_table, expert_total):
    flat_ids = id_table.reshape(-1)
    onehot = (flat_ids[:, None] == jnp.arange(expert_total, dtype=jnp.int32)[None, :]).astype(
        jnp.int32
    )
    before = jnp.cumsum(onehot, axis=0) - onehot
    return jnp.sum(before * onehot, axis=1).reshape(id_table.shape)


def body(tokens, norm_gain, expert_ids, route_weights, gate_proj, up_proj, down_proj):
    dp_count = lax.axis_size("dp")
    expert_count = lax.axis_size("expert")
    local_experts = gate_proj.shape[0]
    model_width = tokens.shape[2]
    group_ids = expert_ids[0]
    group_weights = route_weights[0]
    group_size = group_ids.shape[0]
    own_rows = group_size // dp_count
    top_k = group_ids.shape[1]
    experts = local_experts * expert_count
    capacity = dp_count * (group_size * top_k // (experts * dp_count) + 1)
    tok_float = tokens[0].astype(jnp.float32)
    inv_rms = lax.rsqrt(jnp.mean(tok_float * tok_float, axis=-1, keepdims=True) + 1e-06)
    group_rows = (tok_float * inv_rms * norm_gain).astype(jnp.bfloat16)
    slot_rank = rank_slots(group_ids, experts)
    slot_index = group_ids * capacity + slot_rank
    token_order = jnp.broadcast_to(
        jnp.arange(group_size, dtype=jnp.int32)[:, None], (group_size, top_k)
    )
    sources = (
        jnp.full((experts * capacity,), group_size, jnp.int32)
        .at[slot_index.reshape(-1)]
        .set(token_order.reshape(-1))
    )
    padded = jnp.concatenate([group_rows, jnp.zeros((1, model_width), jnp.bfloat16)], axis=0)
    outgoing = jnp.take(padded, sources, axis=0).reshape(
        expert_count, local_experts, capacity, model_width
    )
    incoming = lax.all_to_all(outgoing, "expert", split_axis=0, concat_axis=0, tiled=True)
    gate_act = jnp.einsum("sjmd,jfd->sjmf", incoming, gate_proj, preferred_element_type=jnp.float32)
    up_act = jnp.einsum("sjmd,jfd->sjmf", incoming, up_proj, preferred_element_type=jnp.float32)
    hidden = (jax.nn.silu(gate_act) * up_act).astype(jnp.bfloat16)
    partial_rows = jnp.einsum(
        "sjmf,jfd->sjmd", hidden, down_proj, preferred_element_type=jnp.float32
    ).astype(jnp.bfloat16)
    returned = lax.all_to_all(partial_rows, "expert", split_axis=0, concat_axis=0, tiled=True)
    lookup = jnp.concatenate(
        [
            returned.reshape(experts * capacity, model_width),
            jnp.zeros((1, model_width), jnp.bfloat16),
        ],
        axis=0,
    )
    picked = (
        jnp.take(lookup, slot_index.reshape(-1), axis=0)
        .reshape(own_rows * lax.axis_size("dp"), top_k, model_width)
        .astype(jnp.float32)
    )
    mixed = lax.psum_scatter(
        jnp.sum(picked * group_weights[:, :, None], axis=1).astype(jnp.bfloat16),
        "dp",
        scatter_dimension=0,
        tiled=True,
    )
    return mixed[None]


def solution(mesh):
    placed = (
        P("expert", None, None),
        P(),
        P("expert", None, None),
        P("expert", None, None),
        P("expert", "dp", None),
        P("expert", "dp", None),
        P("expert", "dp", None),
    )
    small = mesh.shape["expert"] == 8 and mesh.shape["dp"] == 4
    return jax.shard_map(
        fused_body if small else body, mesh=mesh, in_specs=placed, out_specs=P("expert", "dp", None), check_vma=False
    )
```
